256 devices in a mesh: tile: 32 (over z, y_hi, core), kern: 8 (over x, y_lo).
Axes of the slice: x: 4, y: 4 (y_hi: 2, y_lo: 2; y = y_hi * 2 + y_lo), z: 8, core: 2. Of those that a mesh axis runs over, the one named last changes fastest.
Arguments:
- mask_field: float32 [128, 32768], P(None, 'tile'), may hold values from 0 to 1
- target_image: int32 [128, 32768], P(None, 'tile'), may hold values 0 or 1
- kernels: float32 [24, 2, 61, 61], P('kern'), may hold values from -0.09375 to 0.09375
- kernel_weights: float32 [24], P('kern'), may hold values from 0.01 to 0.1
- live_list: int32 [32, 2], P('tile'), may hold values from 0 to 1, as said below
- live_count: int32 [32], P('tile'), may hold values from 1 to 2, as said below
Outputs:
- gradient: float32 [128, 32768], P('kern', 'tile')
The draws below stay inside these ranges and needn't reach their ends.
Inputs may be any that keep to these rules, and one draw needn't show every extreme that they name: `live_count`: every strip has at least one non-empty tile and some strip has all 2 slots non-empty. `live_list`: each row is a permutation of the slots 0 to 1; its first live_count entries are the strip's non-empty slots in increasing order.
All inputs are finite; a program needn't handle non-finite values. No bound on the sum of `target_image` on one device may be relied on, other than what follows from the above.
Results may differ from the reference program's by a relative error of at most 0.00015.
Values sent between devices are 32-bit elements; how exact they have to be, the bound alone decides.
A program may use at most 128 MiB of HBM per device.

```python
import math
import jax
import jax.numpy as jnp
from jax import lax

TR = 2
KSUP = 61
NK = 24
STRIPS = 32
ROWS = 128
COLS = 32768


def tile_counts(key):
    count_key, full_key = jax.random.split(jax.random.fold_in(key, 11))
    counts = 1 + jax.random.randint(count_key, (STRIPS,), 0, TR // 2 + 1)
    fullest = jax.random.randint(full_key, (), 0, STRIPS)
    return jnp.where(jnp.arange(STRIPS) == fullest, TR, counts).astype(jnp.int32)


def draw_live_count(key, part):
    return tile_counts(key)


def pick_order(subkey):
    return jax.random.permutation(subkey, TR)


def draw_live_list(key, part):
    counts = tile_counts(key)
    key = jax.random.fold_in(key, 7)
    key_list = jax.random.split(key, STRIPS)
    orders = jax.vmap(pick_order)(key_list)
    chosen = orders < counts[:, None]
    scores = jnp.where(chosen, 0, TR) + jnp.arange(TR)[None, :]
    return jnp.argsort(scores, axis=1).astype(jnp.int32)


def with_ends(result, own_key, least, high):
    longest = result.shape.index(max(result.shape))
    spots = []
    for shift in (0, 1):
        where = [jax.random.randint(jax.random.fold_in(own_key, axis), (), 0, length) for axis, length in enumerate(result.shape)]
        where[longest] = (where[longest] + shift) % result.shape[longest]
        spots.append(tuple(where))
    return result.at[spots[0]].set(least).at[spots[1]].set(high)


def steps_of(key, shape, shards, least, top_value):
    gain = 1.0
    for position, parts in shards:
        heights = jax.random.uniform(jax.random.fold_in(jax.random.fold_in(key, 6), position), (parts,), jnp.float32, least / len(shards), top_value / len(shards))
        gain = gain * jnp.repeat(jnp.exp(heights), shape[position] // parts).reshape((-1,) + (1,) * (len(shape) - 1 - position))
    return gain


def bell_draw(stream_key, dims, spread, bound, pieces=(), kind=jnp.bfloat16):
    gain = steps_of(stream_key, dims, pieces, -0.22, 0.18) if pieces else 1.0
    drawn = jax.random.normal(stream_key, dims, jnp.float32) * spread * gain
    return jnp.minimum(jnp.maximum(drawn, -bound), bound).astype(kind)


def setup_inputs(seed: int = 0) -> dict:
    key_of = jax.random.split(jax.random.key(seed), 7)
    mask_field = jnp.clip(1.0 * jax.random.uniform(key_of[0], (ROWS, COLS), jnp.float32) ** steps_of(key_of[0], (ROWS, COLS), ((1, 32),), -0.2, 0.2), 0.0, 1.0)
    target_image = with_ends((jax.random.randint(key_of[1], (ROWS, COLS), 0, 2) < 1).astype(jnp.int32), jax.random.fold_in(key_of[1], 1), 0, 1)
    kernels = bell_draw(key_of[2], (NK, 2, KSUP, KSUP), (KSUP * KSUP) ** -0.5, 0.09375, ((0, 8),), jnp.float32)
    kernel_weights = jnp.clip(jnp.exp(math.log(0.1) - 2.3025851 * jax.random.uniform(key_of[3], (NK,), jnp.float32) ** steps_of(key_of[3], (NK,), ((0, 8),), -0.2, 0.2)), 0.01, 0.1)
    live_list = draw_live_list(jax.random.fold_in(key_of[6], 71), 0)
    live_count = draw_live_count(jax.random.fold_in(key_of[6], 71), 0)
    return dict(mask_field=mask_field, target_image=target_image, kernels=kernels, kernel_weights=kernel_weights, live_list=live_list, live_count=live_count)


steepness = 4.0
threshold = 0.6


def round_up(value, step):
    return ((value + step - 1) // step) * step


def reference(mask_field, target_image, kernels, kernel_weights, live_list, live_count):
    strip_rows, chip_cols = mask_field.shape
    slot_count = live_list.shape[1]
    tile_rows = strip_rows // slot_count
    tile_cols = chip_cols // live_list.shape[0]
    rim_width = (KSUP - 1) // 2
    slot_ids = jnp.arange(slot_count, dtype=jnp.int32)
    matches = (live_list[:, :, None] == slot_ids[None, None, :]) & (slot_ids[None, :, None] < live_count[:, None, None])
    tile_flags = jnp.any(matches, axis=1).astype(mask_field.dtype)
    live_pixels = jnp.repeat(jnp.repeat(tile_flags.T, tile_rows, axis=0), tile_cols, axis=1)
    masked = mask_field * live_pixels
    padded_rows = round_up(strip_rows + 2 * rim_width, 64)
    padded_cols = round_up(chip_cols + 2 * rim_width, 1024)
    mask_hat = jnp.fft.fft2(jnp.pad(masked, ((0, padded_rows - strip_rows), (0, padded_cols - chip_cols))))

    def spectrum(kernel):
        placed = jnp.pad(kernel[0] + 1j * kernel[1], ((0, padded_rows - KSUP), (0, padded_cols - KSUP)))
        return jnp.fft.fft2(jnp.roll(placed, (-rim_width, -rim_width), axis=(0, 1)))

    def kernel_field(kernel):
        return jnp.fft.ifft2(mask_hat * spectrum(kernel))[:strip_rows, :chip_cols]

    def add_power(running, operand):
        kernel, weight = operand
        field_value = kernel_field(kernel)
        field_real = jnp.real(field_value)
        field_imag = jnp.imag(field_value)
        return running + weight * (field_real * field_real + field_imag * field_imag), None

    intensity, unused = lax.scan(add_power, jnp.zeros_like(masked), (kernels, kernel_weights))
    printed = jax.nn.sigmoid(steepness * (intensity - threshold))
    loss_slope = live_pixels * 2.0 * steepness * (printed - target_image.astype(masked.dtype)) * printed * (1.0 - printed)

    def add_adjoint(running, operand):
        kernel, weight = operand
        field_value = kernel_field(kernel)
        source = jnp.pad(loss_slope * field_value, ((0, padded_rows - strip_rows), (0, padded_cols - chip_cols)))
        return running + 2.0 * weight * jnp.fft.fft2(source) * jnp.conj(spectrum(kernel)), None

    accumulated, unused = lax.scan(add_adjoint, jnp.zeros(mask_hat.shape, mask_hat.dtype), (kernels, kernel_weights))
    gradient = jnp.real(jnp.fft.ifft2(accumulated))[:strip_rows, :chip_cols] * live_pixels
    return gradient
```

```python
import functools

import jax
import jax.numpy as jnp
import ml_dtypes
import numpy as np
from jax import lax
from jax.experimental import pallas as pl
from jax.experimental.pallas import tpu as pltpu
from jax.sharding import PartitionSpec as P

MESH = pl.DeviceIdType.MESH
steepness = 4.0
threshold = 0.6

ROWS = 128
BLOCK = 128
RIM = 30
SUP = 61
PERIOD_R = 159
FREQ_R = 80
PERIOD_C = 255
FREQ_C = 128
SIDE = 64


def split_np(table):
    hi = table.astype(np.float32).astype(ml_dtypes.bfloat16)
    lo = (table - hi.astype(np.float64)).astype(np.float32).astype(ml_dtypes.bfloat16)
    return hi, lo


def phases(first, second, period):
    angle = 2.0 * np.pi / period * (np.outer(first, second) % period)
    return np.cos(angle), np.sin(angle)


@functools.cache
def tables():
    fr, fc = np.arange(FREQ_R), np.arange(FREQ_C)
    rows, window = np.arange(ROWS), np.arange(2 * BLOCK)
    taps = np.arange(SUP) - RIM
    row_weight = np.where(fr == 0, 1.0, 2.0) / PERIOD_R
    col_weight = np.where(fc == 0, 1.0, 2.0) / PERIOD_C * 0.5
    c, s = phases(fr, rows, PERIOD_R)
    to_rows_hi, to_rows_lo = split_np(np.concatenate([c, s], 0))
    row_forward = np.concatenate([to_rows_hi, to_rows_hi, to_rows_lo], 1)
    back = np.concatenate([c * row_weight[:, None], s * row_weight[:, None]], 0).T
    back_hi, back_lo = split_np(back)
    row_back = np.concatenate([back_hi, back_hi, back_lo], 1)
    c, s = phases(window, fc, PERIOD_C)
    col_hi, col_lo = split_np(np.concatenate([c, s], 1))
    inv = np.concatenate([(c * col_weight).T, (s * col_weight).T], 0)
    inv_hi, inv_lo = split_np(inv)
    mid = slice(SIDE, SIDE + BLOCK)
    inv_mid = np.concatenate([inv_hi[:, mid], inv_lo[:, mid]], 1)
    src_hi = np.concatenate([col_hi[mid], col_hi[mid], col_lo[mid]], 0)
    c, s = phases(taps, fc, PERIOD_C)
    tap_cols = np.zeros((64, 2 * FREQ_C))
    tap_cols[:SUP] = np.concatenate([c, s], 1)
    tc_hi, tc_lo = split_np(tap_cols)
    zero = np.zeros_like(tc_hi)

    def pair(t):
        return np.concatenate(
            [np.concatenate([t, zero], 1), np.concatenate([zero, t], 1)], 0
        )

    tap_col = np.concatenate([pair(tc_hi), pair(tc_hi), pair(tc_lo)], 0)
    c, s = phases(fr, taps, PERIOD_R)
    tap_rows = np.zeros((2 * FREQ_R, 64))
    tap_rows[:, :SUP] = np.concatenate([c, s], 0)
    tr_hi, tr_lo = split_np(tap_rows)
    tap_row = np.concatenate([tr_hi, tr_hi, tr_lo], 1)
    return (row_forward, row_back, col_hi, col_lo, inv_hi, inv_lo, inv_mid, src_hi, tap_col, tap_row)


def split(value):
    hi = value.astype(jnp.bfloat16)
    lo = (value - hi.astype(jnp.float32)).astype(jnp.bfloat16)
    return hi, lo


def dot(a, b):
    return jnp.dot(a, b, preferred_element_type=jnp.float32)


def dot3(a, b_hi, b_lo):
    a_hi, a_lo = split(a)
    return dot(a_hi, b_hi) + (dot(a_lo, b_hi) + dot(a_hi, b_lo))


def stacked(value):
    hi, lo = split(value)
    return jnp.concatenate([hi, lo, hi], 0)


def quarters(spec):
    cc, cs = spec[:FREQ_R, :FREQ_C], spec[:FREQ_R, FREQ_C:]
    sc, ss = spec[FREQ_R:, :FREQ_C], spec[FREQ_R:, FREQ_C:]
    return cc - ss, cs + sc, cc + ss, sc - cs


def unquarters(ur, ui, vr, vi):
    top = jnp.concatenate([ur + vr, ui - vi], 1)
    bottom = jnp.concatenate([ui + vi, vr - ur], 1)
    return jnp.concatenate([top, bottom], 0)


def body(
    strips, parts, local,
    mask_ref, target_ref, kern_ref, weight_ref, list_ref, count_ref,
    row_forward, row_back, col_hi, col_lo, inv_hi, inv_lo, inv_mid, src_tab, tap_col, tap_row,
    out_ref,
    kbuf, halo_src, halo_left, halo_right, xspec, spec, fields, inten, gspec, gwin, rbuf, edge_left, edge_right, acc,
    k_send, k_recv, h_send, h_recv, g_send, g_recv, e_send, e_recv,
):
    t = lax.axis_index("tile")
    j = lax.axis_index("kern")
    up = lax.rem(t + 1, strips)
    down = lax.rem(t + strips - 1, strips)
    chunk = ROWS // parts
    first, last = j == 0, j == parts - 1

    barrier = pltpu.get_barrier_semaphore()
    for d in range(1, parts):
        pl.semaphore_signal(barrier, inc=1, device_id=(t, lax.rem(j + d, parts)), device_id_type=MESH)
    pl.semaphore_signal(barrier, inc=1, device_id=(up, 0), device_id_type=MESH)
    pl.semaphore_signal(barrier, inc=1, device_id=(down, parts - 1), device_id_type=MESH)

    kbuf[0] = jnp.zeros_like(kbuf[0])
    for k in range(local):
        kbuf[0, 64 * k : 64 * k + SUP, 0:SUP] = kern_ref[k, 0]
        kbuf[0, 64 * k : 64 * k + SUP, 64 : 64 + SUP] = kern_ref[k, 1]
        kbuf[0, 64 * k + SUP : 64 * k + SUP + 1, :] = jnp.full((1, 128), weight_ref[k], jnp.float32)

    def flag(slot):
        found = jnp.float32(0.0)
        for place in range(2):
            hit = (list_ref[0, place] == slot) & (place < count_ref[0])
            found = jnp.where(hit, jnp.float32(1.0), found)
        return found

    half = ROWS // 2
    live_rows = jnp.concatenate(
        [jnp.full((half, 128), flag(0), jnp.float32), jnp.full((half, 128), flag(1), jnp.float32)], 0
    )

    def column(index):
        return mask_ref[:, pl.ds(pl.multiple_of(index * 128, 128), 128)] * live_rows

    halo_src[...] = jnp.where(first, column(0), column(parts - 1))

    @pl.when(first)
    def _():
        pl.semaphore_wait(barrier, 2 * parts - 1)

    @pl.when(last)
    def _():
        pl.semaphore_wait(barrier, 2 * parts - 1)

    @pl.when(jnp.logical_not(first | last))
    def _():
        pl.semaphore_wait(barrier, parts - 1)

    def to_down():
        return pltpu.make_async_remote_copy(
            halo_src, halo_right, h_send.at[0], h_recv.at[0],
            device_id=(down, parts - 1), device_id_type=MESH)

    def to_up():
        return pltpu.make_async_remote_copy(
            halo_src, halo_left, h_send.at[0], h_recv.at[0],
            device_id=(up, 0), device_id_type=MESH)

    @pl.when(first)
    def _():
        to_down().start()

    @pl.when(last)
    def _():
        to_up().start()

    def kern_copy(d):
        return pltpu.make_async_remote_copy(
            kbuf.at[0], kbuf.at[d], k_send.at[d], k_recv.at[d],
            device_id=(t, lax.rem(j + d, parts)), device_id_type=MESH)

    for d in range(1, parts):
        kern_copy(d).start()

    @pl.when(first)
    def _():
        to_down().wait()

    @pl.when(last)
    def _():
        to_up().wait()

    before = jnp.where(
        first,
        jnp.where(t > 0, halo_left[...], 0.0),
        column(jnp.maximum(j - 1, 0)),
    )
    after = jnp.where(
        last,
        jnp.where(t < strips - 1, halo_right[...], 0.0),
        column(jnp.minimum(j + 1, parts - 1)),
    )
    here = column(j)
    window = jnp.concatenate([before[:, SIDE:], here, after[:, :SIDE]], 1)
    by_rows = dot(row_forward[...], stacked(window))
    spectrum = dot3(by_rows, col_hi[...], col_lo[...])
    for place, piece in enumerate(quarters(spectrum)):
        xspec[place] = piece

    inten[...] = jnp.zeros_like(inten)

    def forward(d, carry):
        @pl.when(d > 0)
        def _():
            kern_copy(d).wait()

        k_hi, k_lo = split(kbuf[d])
        taps = dot(jnp.concatenate([k_hi, k_lo], 1), tap_col[0:256, :]) + dot(k_hi, tap_col[256:384, :])
        t_hi, t_lo = split(taps)
        for k in range(local):
            place = d * local + k
            rows = slice(64 * k, 64 * k + 64)
            both = dot(tap_row[...], jnp.concatenate([t_hi[rows], t_lo[rows], t_hi[rows]], 0))
            products = []
            for part in range(2):
                lanes = slice(part * 128, part * 128 + 128)
                ur, ui, vr, vi = quarters(both[:, part * 256 : part * 256 + 256])
                spec[place, 0, :, lanes] = ur
                spec[place, 1, :, lanes] = ui
                spec[place, 2, :, lanes] = vr
                spec[place, 3, :, lanes] = vi
                xur, xui, xvr, xvi = xspec[0], xspec[1], xspec[2], xspec[3]
                products.append(
                    unquarters(
                        ur * xur - ui * xui, ur * xui + ui * xur,
                        vr * xvr - vi * xvi, vr * xvi + vi * xvr,
                    )
                )
            y_hi, y_lo = split(jnp.concatenate(products, 0))
            wide = dot(y_hi, inv_mid[...])
            inner = wide[:, :128] + (wide[:, 128:] + dot(y_lo, inv_mid[:, :128]))
            n = 2 * FREQ_R
            field = dot(row_back[...], stacked(jnp.concatenate([inner[:n], inner[n:]], 1)))
            fields[place] = field
            weight = kbuf[d, 64 * k + SUP : 64 * k + SUP + 1, :]
            real, imag = field[:, :128], field[:, 128:]
            inten[...] += weight * (real * real + imag * imag)
        return carry

    lax.fori_loop(0, parts, forward, 0)

    printed = jax.nn.sigmoid(steepness * (inten[...] - threshold))
    target = target_ref[:, pl.ds(pl.multiple_of(j * 128, 128), 128)].astype(jnp.float32)
    inten[...] = live_rows * (4.0 * steepness) * (printed - target) * printed * (1.0 - printed)
    gspec[...] = jnp.zeros_like(gspec)

    def adjoint(d, carry):
        for k in range(local):
            place = d * local + k
            weight = kbuf[d, 64 * k + SUP : 64 * k + SUP + 1, :]
            slope = inten[...] * weight
            source = fields[place] * jnp.concatenate([slope, slope], 1)
            by_rows = dot(row_forward[...], stacked(source))
            pair = jnp.concatenate([by_rows[:, :128], by_rows[:, 128:]], 0)
            s_hi, s_lo = split(pair)
            found = dot(jnp.concatenate([s_hi, s_lo], 1), src_tab[0:256, :]) + dot(s_hi, src_tab[256:384, :])
            n = 2 * FREQ_R
            for part in range(2):
                lanes = slice(part * 128, part * 128 + 128)
                sur, sui, svr, svi = quarters(found[part * n : part * n + n])
                ur, ui = spec[place, 0, :, lanes], spec[place, 1, :, lanes]
                vr, vi = spec[place, 2, :, lanes], spec[place, 3, :, lanes]
                gspec[0] += sur * ur + sui * ui
                gspec[1] += sui * ur - sur * ui
                gspec[2] += svr * vr + svi * vi
                gspec[3] += svi * vr - svr * vi
        return carry

    lax.fori_loop(0, parts, adjoint, 0)

    total = unquarters(gspec[0], gspec[1], gspec[2], gspec[3])
    inner = dot3(total, inv_hi[...], inv_lo[...])
    gwin[...] = dot(row_back[...], stacked(inner))

    def rows_of(index):
        return pl.ds(pl.multiple_of(index * chunk, chunk), chunk)

    def grad_copy(d):
        other = lax.rem(j + d, parts)
        return pltpu.make_async_remote_copy(
            gwin.at[rows_of(other), :], rbuf.at[d], g_send.at[d], g_recv.at[d],
            device_id=(t, other), device_id_type=MESH)

    def edge_down(i):
        return pltpu.make_async_remote_copy(
            gwin.at[i * chunk : (i + 1) * chunk, 0:128], edge_right, e_send.at[i], e_recv.at[0],
            device_id=(down, i), device_id_type=MESH)

    def edge_up(i):
        return pltpu.make_async_remote_copy(
            gwin.at[i * chunk : (i + 1) * chunk, 128:256], edge_left, e_send.at[i], e_recv.at[1],
            device_id=(up, i), device_id_type=MESH)

    @pl.when(first)
    def _():
        for i in range(parts):
            edge_down(i).start()

    @pl.when(last)
    def _():
        for i in range(parts):
            edge_up(i).start()

    for d in range(1, parts):
        grad_copy(d).start()

    acc[...] = jnp.zeros_like(acc)
    acc[:, pl.ds(pl.multiple_of(j * 128, 128), 256)] += gwin[rows_of(j), :]
    for d in range(1, parts):
        grad_copy(d).wait_recv()
        source = lax.rem(j + parts - d, parts)
        acc[:, pl.ds(pl.multiple_of(source * 128, 128), 256)] += rbuf[d]
    edge_down(0).wait_recv()
    edge_up(0).wait_recv()
    acc[:, BLOCK * parts :] += jnp.where(t < strips - 1, edge_right[...], 0.0)
    acc[:, 0:128] += jnp.where(t > 0, edge_left[...], 0.0)
    half_parts = parts // 2
    mine = jnp.where(j < half_parts, flag(0), flag(1))
    out_ref[...] = acc[:, SIDE : SIDE + BLOCK * parts] * mine

    for d in range(1, parts):
        grad_copy(d).wait_send()

    @pl.when(first)
    def _():
        for i in range(parts):
            edge_down(i).wait_send()

    @pl.when(last)
    def _():
        for i in range(parts):
            edge_up(i).wait_send()


def shards(mask_field, target_image, kernels, kernel_weights, live_list, live_count):
    strips, parts = lax.axis_size("tile"), lax.axis_size("kern")
    local = kernels.shape[0]
    count = local * parts
    vmem = pl.BlockSpec(memory_space=pltpu.VMEM)
    smem = pl.BlockSpec(memory_space=pltpu.SMEM)
    f32 = jnp.float32
    chunk = ROWS // parts
    consts = tables()
    return pl.pallas_call(
        functools.partial(body, strips, parts, local),
        out_shape=jax.ShapeDtypeStruct((chunk, BLOCK * parts), f32),
        in_specs=[vmem, vmem, vmem, smem, smem, smem] + [vmem] * len(consts),
        out_specs=vmem,
        scratch_shapes=[
            pltpu.VMEM((parts, 64 * local, 128), f32),
            pltpu.VMEM((ROWS, 128), f32),
            pltpu.VMEM((ROWS, 128), f32),
            pltpu.VMEM((ROWS, 128), f32),
            pltpu.VMEM((4, FREQ_R, FREQ_C), f32),
            pltpu.VMEM((count, 4, FREQ_R, 2 * FREQ_C), f32),
            pltpu.VMEM((count, ROWS, 256), f32),
            pltpu.VMEM((ROWS, 128), f32),
            pltpu.VMEM((4, FREQ_R, FREQ_C), f32),
            pltpu.VMEM((ROWS, 256), f32),
            pltpu.VMEM((parts, chunk, 256), f32),
            pltpu.VMEM((chunk, 128), f32),
            pltpu.VMEM((chunk, 128), f32),
            pltpu.VMEM((chunk, BLOCK * parts + 128), f32),
            pltpu.SemaphoreType.DMA((parts,)),
            pltpu.SemaphoreType.DMA((parts,)),
            pltpu.SemaphoreType.DMA((1,)),
            pltpu.SemaphoreType.DMA((1,)),
            pltpu.SemaphoreType.DMA((parts,)),
            pltpu.SemaphoreType.DMA((parts,)),
            pltpu.SemaphoreType.DMA((parts,)),
            pltpu.SemaphoreType.DMA((2,)),
        ],
        compiler_params=pltpu.CompilerParams(
            collective_id=0, has_side_effects=True, vmem_limit_bytes=56 * 1024 * 1024
        ),
    )(mask_field, target_image, kernels, kernel_weights, live_list, live_count, *consts)


def solution(mesh):
    placed = (
        P(None, "tile"),
        P(None, "tile"),
        P("kern", None, None, None),
        P("kern"),
        P("tile", None),
        P("tile"),
    )
    return jax.shard_map(
        shards, mesh=mesh, in_specs=placed, out_specs=P("kern", "tile"), check_vma=False
    )
```

```python
import functools

import jax
import jax.numpy as jnp
import ml_dtypes
import numpy as np
from jax import lax
from jax.experimental import pallas as pl
from jax.experimental.pallas import tpu as pltpu
from jax.sharding import PartitionSpec as P

MESH = pl.DeviceIdType.MESH
steepness = 4.0
threshold = 0.6

ROWS = 128
BLOCK = 128
RIM = 30
SUP = 61
PERIOD_R = 159
FREQ_R = 80
PERIOD_C = 255
FREQ_C = 128
SIDE = 64


def split_np(table):
    hi = table.astype(np.float32).astype(ml_dtypes.bfloat16)
    lo = (table - hi.astype(np.float64)).astype(np.float32).astype(ml_dtypes.bfloat16)
    return hi, lo


def phases(first, second, period):
    angle = 2.0 * np.pi / period * (np.outer(first, second) % period)
    return np.cos(angle), np.sin(angle)


@functools.cache
def tables():
    fr, fc = np.arange(FREQ_R), np.arange(FREQ_C)
    rows, window = np.arange(ROWS), np.arange(2 * BLOCK)
    taps = np.arange(SUP) - RIM
    row_weight = np.where(fr == 0, 1.0, 2.0) / PERIOD_R
    col_weight = np.where(fc == 0, 1.0, 2.0) / PERIOD_C * 0.5
    c, s = phases(fr, rows, PERIOD_R)
    to_rows_hi, to_rows_lo = split_np(np.concatenate([c, s], 0))
    row_forward = np.concatenate([to_rows_hi, to_rows_hi, to_rows_lo], 1)
    back = np.concatenate([c * row_weight[:, None], s * row_weight[:, None]], 0).T
    back_hi, back_lo = split_np(back)
    row_back = np.concatenate([back_hi, back_hi, back_lo], 1)
    c, s = phases(window, fc, PERIOD_C)
    col_hi, col_lo = split_np(np.concatenate([c, s], 1))
    inv = np.concatenate([(c * col_weight).T, (s * col_weight).T], 0)
    inv_hi, inv_lo = split_np(inv)
    mid = slice(SIDE, SIDE + BLOCK)
    inv_mid = np.concatenate([inv_hi[:, mid], inv_lo[:, mid]], 1)
    src_hi = np.concatenate([col_hi[mid], col_hi[mid], col_lo[mid]], 0)
    c, s = phases(taps, fc, PERIOD_C)
    tap_cols = np.zeros((64, 2 * FREQ_C))
    tap_cols[:SUP] = np.concatenate([c, s], 1)
    tc_hi, tc_lo = split_np(tap_cols)
    zero = np.zeros_like(tc_hi)

    def pair(t):
        return np.concatenate(
            [np.concatenate([t, zero], 1), np.concatenate([zero, t], 1)], 0
        )

    tap_col = np.concatenate([pair(tc_hi), pair(tc_hi), pair(tc_lo)], 0)
    c, s = phases(fr, taps, PERIOD_R)
    tap_rows = np.zeros((2 * FREQ_R, 64))
    tap_rows[:, :SUP] = np.concatenate([c, s], 0)
    tr_hi, tr_lo = split_np(tap_rows)
    tap_row = np.concatenate([tr_hi, tr_hi, tr_lo], 1)
    return (row_forward, row_back, col_hi, col_lo, inv_hi, inv_lo, inv_mid, src_hi, tap_col, tap_row)


def split(value):
    hi = value.astype(jnp.bfloat16)
    lo = (value - hi.astype(jnp.float32)).astype(jnp.bfloat16)
    return hi, lo


def dot(a, b):
    return jnp.dot(a, b, preferred_element_type=jnp.float32)


def dot3(a, b_hi, b_lo):
    a_hi, a_lo = split(a)
    return dot(a_hi, b_hi) + (dot(a_lo, b_hi) + dot(a_hi, b_lo))


def stacked(value):
    hi, lo = split(value)
    return jnp.concatenate([hi, lo, hi], 0)


def quarters(spec):
    cc, cs = spec[:FREQ_R, :FREQ_C], spec[:FREQ_R, FREQ_C:]
    sc, ss = spec[FREQ_R:, :FREQ_C], spec[FREQ_R:, FREQ_C:]
    return cc - ss, cs + sc, cc + ss, sc - cs


def unquarters(ur, ui, vr, vi):
    top = jnp.concatenate([ur + vr, ui - vi], 1)
    bottom = jnp.concatenate([ui + vi, vr - ur], 1)
    return jnp.concatenate([top, bottom], 0)


def body(
    strips, parts, local,
    mask_ref, target_ref, kern_ref, weight_ref, list_ref, count_ref, *rest,
):
    table_count = len(tables())
    in_hbm, rest = rest[:table_count], rest[table_count:]
    out_ref, rest = rest[0], rest[1:]
    held, rest = rest[:table_count], rest[table_count:]
    run(strips, parts, local, mask_ref, target_ref, kern_ref, weight_ref, list_ref, count_ref, in_hbm, out_ref, held, *rest)


def run(
    strips, parts, local,
    mask_ref, target_ref, kern_ref, weight_ref, list_ref, count_ref, in_hbm, out_ref, held,
    raw, mwin, twin, l_sem, t_sem,
    kbuf, halo_src, halo_left, halo_right, xspec, spec, fields, inten, gspec, gwin, rbuf, edge_left, edge_right, acc,
    k_send, k_recv, h_send, h_recv, g_send, g_recv, e_send, e_recv,
):
    t = lax.axis_index("tile")
    j = lax.axis_index("kern")
    up = lax.rem(t + 1, strips)
    down = lax.rem(t + strips - 1, strips)
    chunk = ROWS // parts
    first, last = j == 0, j == parts - 1
    has_up, has_down = t < strips - 1, t > 0
    sends_up, sends_down = last & has_up, first & has_down
    row_forward, row_back, col_hi, col_lo, inv_hi, inv_lo, inv_mid, src_tab, tap_col, tap_row = held

    def strip_column(ref, index):
        return ref.at[:, pl.ds(pl.multiple_of(index * 128, 128), 128)]

    kern_load = pltpu.make_async_copy(kern_ref, raw, l_sem.at[0])
    kern_load.start()
    loads = [
        pltpu.make_async_copy(strip_column(mask_ref, j), mwin.at[1], l_sem.at[2]),
        pltpu.make_async_copy(strip_column(mask_ref, jnp.maximum(j - 1, 0)), mwin.at[0], l_sem.at[1]),
        pltpu.make_async_copy(strip_column(mask_ref, jnp.minimum(j + 1, parts - 1)), mwin.at[2], l_sem.at[3]),
        pltpu.make_async_copy(strip_column(target_ref, j), twin, l_sem.at[4]),
    ]
    for load in loads:
        load.start()
    table_loads = [
        pltpu.make_async_copy(source, place, t_sem.at[i]) for i, (source, place) in enumerate(zip(in_hbm, held))
    ]
    for load in table_loads:
        load.start()

    barrier = pltpu.get_barrier_semaphore()
    for d in range(1, parts):
        pl.semaphore_signal(barrier, inc=1, device_id=(t, lax.rem(j + d, parts)), device_id_type=MESH)

    @pl.when(has_up)
    def _():
        pl.semaphore_signal(barrier, inc=1, device_id=(up, 0), device_id_type=MESH)

    @pl.when(has_down)
    def _():
        pl.semaphore_signal(barrier, inc=1, device_id=(down, parts - 1), device_id_type=MESH)

    kbuf[0] = jnp.zeros_like(kbuf[0])
    kern_load.wait()
    for k in range(local):
        kbuf[0, 64 * k : 64 * k + SUP, 0:SUP] = raw[k, 0]
        kbuf[0, 64 * k : 64 * k + SUP, 64 : 64 + SUP] = raw[k, 1]
        kbuf[0, 64 * k + SUP : 64 * k + SUP + 1, :] = jnp.full((1, 128), weight_ref[k], jnp.float32)

    def flag(slot):
        found = jnp.float32(0.0)
        for place in range(2):
            hit = (list_ref[0, place] == slot) & (place < count_ref[0])
            found = jnp.where(hit, jnp.float32(1.0), found)
        return found

    half = ROWS // 2
    live_rows = jnp.concatenate(
        [jnp.full((half, 128), flag(0), jnp.float32), jnp.full((half, 128), flag(1), jnp.float32)], 0
    )

    for load in loads[:3]:
        load.wait()
    here = mwin[1] * live_rows
    halo_src[...] = here

    edge_device = sends_up | sends_down

    @pl.when(edge_device)
    def _():
        pl.semaphore_wait(barrier, 2 * parts - 1)

    @pl.when(jnp.logical_not(edge_device))
    def _():
        pl.semaphore_wait(barrier, parts - 1)

    def to_down():
        return pltpu.make_async_remote_copy(
            halo_src, halo_right, h_send.at[0], h_recv.at[0],
            device_id=(down, parts - 1), device_id_type=MESH)

    def to_up():
        return pltpu.make_async_remote_copy(
            halo_src, halo_left, h_send.at[0], h_recv.at[0],
            device_id=(up, 0), device_id_type=MESH)

    @pl.when(sends_down)
    def _():
        to_down().start()

    @pl.when(sends_up)
    def _():
        to_up().start()

    def kern_copy(d):
        return pltpu.make_async_remote_copy(
            kbuf.at[0], kbuf.at[d], k_send.at[d], k_recv.at[d],
            device_id=(t, lax.rem(j + d, parts)), device_id_type=MESH)

    for d in range(1, parts):
        kern_copy(d).start()

    @pl.when(sends_down)
    def _():
        to_down().wait()

    @pl.when(sends_up)
    def _():
        to_up().wait()

    before = jnp.where(first, jnp.where(has_down, halo_left[...], 0.0), mwin[0] * live_rows)
    after = jnp.where(last, jnp.where(has_up, halo_right[...], 0.0), mwin[2] * live_rows)
    for load in table_loads:
        load.wait()
    window = jnp.concatenate([before[:, SIDE:], here, after[:, :SIDE]], 1)
    by_rows = dot(row_forward[...], stacked(window))
    spectrum = dot3(by_rows, col_hi[...], col_lo[...])
    for place, piece in enumerate(quarters(spectrum)):
        xspec[place] = piece

    inten[...] = jnp.zeros_like(inten)

    def forward(d, carry):
        @pl.when(d > 0)
        def _():
            kern_copy(d).wait()

        k_hi, k_lo = split(kbuf[d])
        taps = dot(jnp.concatenate([k_hi, k_lo], 1), tap_col[0:256, :]) + dot(k_hi, tap_col[256:384, :])
        t_hi, t_lo = split(taps)
        for k in range(local):
            place = d * local + k
            rows = slice(64 * k, 64 * k + 64)
            both = dot(tap_row[...], jnp.concatenate([t_hi[rows], t_lo[rows], t_hi[rows]], 0))
            products = []
            for part in range(2):
                lanes = slice(part * 128, part * 128 + 128)
                ur, ui, vr, vi = quarters(both[:, part * 256 : part * 256 + 256])
                spec[place, 0, :, lanes] = ur
                spec[place, 1, :, lanes] = ui
                spec[place, 2, :, lanes] = vr
                spec[place, 3, :, lanes] = vi
                xur, xui, xvr, xvi = xspec[0], xspec[1], xspec[2], xspec[3]
                products.append(
                    unquarters(
                        ur * xur - ui * xui, ur * xui + ui * xur,
                        vr * xvr - vi * xvi, vr * xvi + vi * xvr,
                    )
                )
            y_hi, y_lo = split(jnp.concatenate(products, 0))
            wide = dot(y_hi, inv_mid[...])
            inner = wide[:, :128] + (wide[:, 128:] + dot(y_lo, inv_mid[:, :128]))
            n = 2 * FREQ_R
            field = dot(row_back[...], stacked(jnp.concatenate([inner[:n], inner[n:]], 1)))
            fields[place] = field
            weight = kbuf[d, 64 * k + SUP : 64 * k + SUP + 1, :]
            real, imag = field[:, :128], field[:, 128:]
            inten[...] += weight * (real * real + imag * imag)
        return carry

    lax.fori_loop(0, parts, forward, 0)

    printed = jax.nn.sigmoid(steepness * (inten[...] - threshold))
    loads[3].wait()
    target = twin[...].astype(jnp.float32)
    inten[...] = live_rows * (4.0 * steepness) * (printed - target) * printed * (1.0 - printed)
    gspec[...] = jnp.zeros_like(gspec)

    def adjoint(d, carry):
        for k in range(local):
            place = d * local + k
            weight = kbuf[d, 64 * k + SUP : 64 * k + SUP + 1, :]
            slope = inten[...] * weight
            source = fields[place] * jnp.concatenate([slope, slope], 1)
            by_rows = dot(row_forward[...], stacked(source))
            pair = jnp.concatenate([by_rows[:, :128], by_rows[:, 128:]], 0)
            s_hi, s_lo = split(pair)
            found = dot(jnp.concatenate([s_hi, s_lo], 1), src_tab[0:256, :]) + dot(s_hi, src_tab[256:384, :])
            n = 2 * FREQ_R
            for part in range(2):
                lanes = slice(part * 128, part * 128 + 128)
                sur, sui, svr, svi = quarters(found[part * n : part * n + n])
                ur, ui = spec[place, 0, :, lanes], spec[place, 1, :, lanes]
                vr, vi = spec[place, 2, :, lanes], spec[place, 3, :, lanes]
                gspec[0] += sur * ur + sui * ui
                gspec[1] += sui * ur - sur * ui
                gspec[2] += svr * vr + svi * vi
                gspec[3] += svi * vr - svr * vi
        return carry

    lax.fori_loop(0, parts, adjoint, 0)

    total = unquarters(gspec[0], gspec[1], gspec[2], gspec[3])
    inner = dot3(total, inv_hi[...], inv_lo[...])
    gwin[...] = dot(row_back[...], stacked(inner))

    def rows_of(index):
        return pl.ds(pl.multiple_of(index * chunk, chunk), chunk)

    def grad_copy(d):
        other = lax.rem(j + d, parts)
        return pltpu.make_async_remote_copy(
            gwin.at[rows_of(other), :], rbuf.at[d], g_send.at[d], g_recv.at[d],
            device_id=(t, other), device_id_type=MESH)

    def edge_down(i):
        return pltpu.make_async_remote_copy(
            gwin.at[i * chunk : (i + 1) * chunk, 0:128], edge_right, e_send.at[i], e_recv.at[0],
            device_id=(down, i), device_id_type=MESH)

    def edge_up(i):
        return pltpu.make_async_remote_copy(
            gwin.at[i * chunk : (i + 1) * chunk, 128:256], edge_left, e_send.at[i], e_recv.at[1],
            device_id=(up, i), device_id_type=MESH)

    @pl.when(sends_down)
    def _():
        for i in range(parts):
            edge_down(i).start()

    @pl.when(sends_up)
    def _():
        for i in range(parts):
            edge_up(i).start()

    for d in range(1, parts):
        grad_copy(d).start()

    acc[...] = jnp.zeros_like(acc)
    acc[:, pl.ds(pl.multiple_of(j * 128, 128), 256)] += gwin[rows_of(j), :]
    for d in range(1, parts):
        grad_copy(d).wait_recv()
        source = lax.rem(j + parts - d, parts)
        acc[:, pl.ds(pl.multiple_of(source * 128, 128), 256)] += rbuf[d]

    @pl.when(has_up)
    def _():
        edge_down(0).wait_recv()
        acc[:, BLOCK * parts :] += edge_right[...]

    @pl.when(has_down)
    def _():
        edge_up(0).wait_recv()
        acc[:, 0:128] += edge_left[...]

    half_parts = parts // 2
    mine = jnp.where(j < half_parts, flag(0), flag(1))
    out_ref[...] = acc[:, SIDE : SIDE + BLOCK * parts] * mine

    for d in range(1, parts):
        grad_copy(d).wait_send()

    @pl.when(sends_down)
    def _():
        for i in range(parts):
            edge_down(i).wait_send()

    @pl.when(sends_up)
    def _():
        for i in range(parts):
            edge_up(i).wait_send()


def shards(mask_field, target_image, kernels, kernel_weights, live_list, live_count):
    strips, parts = lax.axis_size("tile"), lax.axis_size("kern")
    local = kernels.shape[0]
    count = local * parts
    vmem = pl.BlockSpec(memory_space=pltpu.VMEM)
    smem = pl.BlockSpec(memory_space=pltpu.SMEM)
    hbm = pl.BlockSpec(memory_space=pl.ANY)
    f32 = jnp.float32
    chunk = ROWS // parts
    consts = tables()
    return pl.pallas_call(
        functools.partial(body, strips, parts, local),
        out_shape=jax.ShapeDtypeStruct((chunk, BLOCK * parts), f32),
        in_specs=[hbm, hbm, hbm, smem, smem, smem] + [hbm] * len(consts),
        out_specs=vmem,
        scratch_shapes=[pltpu.VMEM(c.shape, jnp.bfloat16) for c in consts]
        + [
            pltpu.VMEM(kernels.shape, f32),
            pltpu.VMEM((3, ROWS, 128), f32),
            pltpu.VMEM((ROWS, 128), jnp.int32),
            pltpu.SemaphoreType.DMA((5,)),
            pltpu.SemaphoreType.DMA((len(consts),)),
            pltpu.VMEM((parts, 64 * local, 128), f32),
            pltpu.VMEM((ROWS, 128), f32),
            pltpu.VMEM((ROWS, 128), f32),
            pltpu.VMEM((ROWS, 128), f32),
            pltpu.VMEM((4, FREQ_R, FREQ_C), f32),
            pltpu.VMEM((count, 4, FREQ_R, 2 * FREQ_C), f32),
            pltpu.VMEM((count, ROWS, 256), f32),
            pltpu.VMEM((ROWS, 128), f32),
            pltpu.VMEM((4, FREQ_R, FREQ_C), f32),
            pltpu.VMEM((ROWS, 256), f32),
            pltpu.VMEM((parts, chunk, 256), f32),
            pltpu.VMEM((chunk, 128), f32),
            pltpu.VMEM((chunk, 128), f32),
            pltpu.VMEM((chunk, BLOCK * parts + 128), f32),
            pltpu.SemaphoreType.DMA((parts,)),
            pltpu.SemaphoreType.DMA((parts,)),
            pltpu.SemaphoreType.DMA((1,)),
            pltpu.SemaphoreType.DMA((1,)),
            pltpu.SemaphoreType.DMA((parts,)),
            pltpu.SemaphoreType.DMA((parts,)),
            pltpu.SemaphoreType.DMA((parts,)),
            pltpu.SemaphoreType.DMA((2,)),
        ],
        compiler_params=pltpu.CompilerParams(
            collective_id=0, has_side_effects=True, vmem_limit_bytes=56 * 1024 * 1024
        ),
    )(mask_field, target_image, kernels, kernel_weights, live_list, live_count, *consts)


def solution(mesh):
    placed = (
        P(None, "tile"),
        P(None, "tile"),
        P("kern", None, None, None),
        P("kern"),
        P("tile", None),
        P("tile"),
    )
    return jax.shard_map(
        shards, mesh=mesh, in_specs=placed, out_specs=P("kern", "tile"), check_vma=False
    )
```

```python
import functools

import jax
import jax.numpy as jnp
import ml_dtypes
import numpy as np
from jax import lax
from jax.experimental import pallas as pl
from jax.experimental.pallas import tpu as pltpu
from jax.sharding import PartitionSpec as P

MESH = pl.DeviceIdType.MESH
steepness = 4.0
threshold = 0.6

ROWS = 128
BLOCK = 128
RIM = 30
SUP = 61
PERIOD_R = 159
FREQ_R = 80
PERIOD_C = 255
FREQ_C = 128
SIDE = 64


def split_np(table):
    hi = table.astype(np.float32).astype(ml_dtypes.bfloat16)
    lo = (table - hi.astype(np.float64)).astype(np.float32).astype(ml_dtypes.bfloat16)
    return hi, lo


def phases(first, second, period):
    angle = 2.0 * np.pi / period * (np.outer(first, second) % period)
    return np.cos(angle), np.sin(angle)


@functools.cache
def tables():
    fr, fc = np.arange(FREQ_R), np.arange(FREQ_C)
    rows, window = np.arange(ROWS), np.arange(2 * BLOCK)
    taps = np.arange(SUP) - RIM
    row_weight = np.where(fr == 0, 1.0, 2.0) / PERIOD_R
    col_weight = np.where(fc == 0, 1.0, 2.0) / PERIOD_C * 0.5
    c, s = phases(fr, rows, PERIOD_R)
    to_rows_hi, to_rows_lo = split_np(np.concatenate([c, s], 0))
    row_forward = np.concatenate([to_rows_hi, to_rows_hi, to_rows_lo], 1)
    back = np.concatenate([c * row_weight[:, None], s * row_weight[:, None]], 0).T
    back_hi, back_lo = split_np(back)
    row_back = np.concatenate([back_hi, back_hi, back_lo], 1)
    c, s = phases(window, fc, PERIOD_C)
    col_hi, col_lo = split_np(np.concatenate([c, s], 1))
    inv = np.concatenate([(c * col_weight).T, (s * col_weight).T], 0)
    inv_hi, inv_lo = split_np(inv)
    mid = slice(SIDE, SIDE + BLOCK)
    inv_mid = np.concatenate([inv_hi[:, mid], inv_lo[:, mid]], 1)
    src_hi = np.concatenate([col_hi[mid], col_hi[mid], col_lo[mid]], 0)
    c, s = phases(taps, fc, PERIOD_C)
    tap_cols = np.zeros((64, 2 * FREQ_C))
    tap_cols[:SUP] = np.concatenate([c, s], 1)
    tc_hi, tc_lo = split_np(tap_cols)
    zero = np.zeros_like(tc_hi)
    tap_real = np.concatenate([tc_hi, tc_hi, tc_lo, zero], 0)
    tap_imag = np.concatenate([tc_hi, tc_hi, zero, tc_lo], 0)
    c, s = phases(fr, taps, PERIOD_R)
    tap_rows = np.zeros((2 * FREQ_R, 64))
    tap_rows[:, :SUP] = np.concatenate([c, s], 0)
    tr_hi, tr_lo = split_np(tap_rows)
    tap_row = np.concatenate([tr_hi, tr_hi, tr_lo], 1)
    return (row_forward, row_back, col_hi, col_lo, inv_hi, inv_lo, inv_mid, src_hi, tap_real, tap_imag, tap_row)


def split(value):
    hi = value.astype(jnp.bfloat16)
    lo = (value - hi.astype(jnp.float32)).astype(jnp.bfloat16)
    return hi, lo


def dot(a, b):
    return jnp.dot(a, b, preferred_element_type=jnp.float32)


def dot3(a, b_hi, b_lo):
    a_hi, a_lo = split(a)
    return dot(a_hi, b_hi) + (dot(a_lo, b_hi) + dot(a_hi, b_lo))


def stacked(value):
    hi, lo = split(value)
    return jnp.concatenate([hi, lo, hi], 0)


def quarters(spec):
    cc, cs = spec[:FREQ_R, :FREQ_C], spec[:FREQ_R, FREQ_C:]
    sc, ss = spec[FREQ_R:, :FREQ_C], spec[FREQ_R:, FREQ_C:]
    return cc - ss, cs + sc, cc + ss, sc - cs


def unquarters(ur, ui, vr, vi):
    top = jnp.concatenate([ur + vr, ui - vi], 1)
    bottom = jnp.concatenate([ui + vi, vr - ur], 1)
    return jnp.concatenate([top, bottom], 0)


def body(
    strips, parts, local,
    mask_ref, target_ref, kern_ref, weight_ref, list_ref, count_ref, *rest,
):
    table_count = len(tables())
    in_hbm, rest = rest[:table_count], rest[table_count:]
    out_ref, rest = rest[0], rest[1:]
    held, rest = rest[:table_count], rest[table_count:]
    run(strips, parts, local, mask_ref, target_ref, kern_ref, weight_ref, list_ref, count_ref, in_hbm, out_ref, held, *rest)


def run(
    strips, parts, local,
    mask_ref, target_ref, kern_ref, weight_ref, list_ref, count_ref, in_hbm, out_ref, held,
    zbuf, sbuf, raw, mwin, twin, l_sem, t_sem,
    kbuf, halo_src, halo_left, halo_right, xspec, spec, fields, inten, gspec, gwin, rbuf, edge_left, edge_right, acc,
    k_send, k_recv, r_send, r_recv, h_send, h_recv, g_send, g_recv, e_send, e_recv,
):
    t = lax.axis_index("tile")
    j = lax.axis_index("kern")
    up = lax.rem(t + 1, strips)
    down = lax.rem(t + strips - 1, strips)
    chunk = ROWS // parts
    first, last = j == 0, j == parts - 1
    has_up, has_down = t < strips - 1, t > 0
    sends_up, sends_down = last & has_up, first & has_down
    row_forward, row_back, col_hi, col_lo, inv_hi, inv_lo, inv_mid, src_tab, tap_real, tap_imag, tap_row = held

    def strip_column(ref, index):
        return ref.at[:, pl.ds(pl.multiple_of(index * 128, 128), 128)]

    kern_load = pltpu.make_async_copy(kern_ref, raw, l_sem.at[0])
    kern_load.start()
    loads = [
        pltpu.make_async_copy(strip_column(mask_ref, j), mwin.at[1], l_sem.at[2]),
        pltpu.make_async_copy(strip_column(mask_ref, jnp.maximum(j - 1, 0)), mwin.at[0], l_sem.at[1]),
        pltpu.make_async_copy(strip_column(mask_ref, jnp.minimum(j + 1, parts - 1)), mwin.at[2], l_sem.at[3]),
        pltpu.make_async_copy(strip_column(target_ref, j), twin, l_sem.at[4]),
    ]
    for load in loads:
        load.start()
    table_loads = [
        pltpu.make_async_copy(source, place, t_sem.at[i]) for i, (source, place) in enumerate(zip(in_hbm, held))
    ]
    for load in table_loads:
        load.start()

    barrier = pltpu.get_barrier_semaphore()
    for d in range(1, parts):
        pl.semaphore_signal(barrier, inc=1, device_id=(t, lax.rem(j + d, parts)), device_id_type=MESH)

    pl.semaphore_signal(barrier, inc=1, device_id=(t + 1 - 2 * lax.rem(t, 2), j), device_id_type=MESH)

    @pl.when(has_up)
    def _():
        pl.semaphore_signal(barrier, inc=1, device_id=(up, 0), device_id_type=MESH)

    @pl.when(has_down)
    def _():
        pl.semaphore_signal(barrier, inc=1, device_id=(down, parts - 1), device_id_type=MESH)

    kbuf[0] = jnp.zeros_like(kbuf[0])
    kern_load.wait()
    for k in range(local):
        kbuf[0, 64 * k : 64 * k + SUP, 0:SUP] = raw[k, :, 0, :]
        kbuf[0, 64 * k : 64 * k + SUP, 64 : 64 + SUP] = raw[k, :, 1, :]
        kbuf[0, 64 * k + SUP : 64 * k + SUP + 1, :] = jnp.full((1, 128), weight_ref[k], jnp.float32)

    def flag(slot):
        found = jnp.float32(0.0)
        for place in range(2):
            hit = (list_ref[0, place] == slot) & (place < count_ref[0])
            found = jnp.where(hit, jnp.float32(1.0), found)
        return found

    half = ROWS // 2
    live_rows = jnp.concatenate(
        [jnp.full((half, 128), flag(0), jnp.float32), jnp.full((half, 128), flag(1), jnp.float32)], 0
    )

    for load in loads[:3]:
        load.wait()
    here = mwin[1] * live_rows
    halo_src[...] = here

    edge_device = sends_up | sends_down

    @pl.when(edge_device)
    def _():
        pl.semaphore_wait(barrier, 2 * parts)

    @pl.when(jnp.logical_not(edge_device))
    def _():
        pl.semaphore_wait(barrier, parts)

    def to_down():
        return pltpu.make_async_remote_copy(
            halo_src, halo_right, h_send.at[0], h_recv.at[0],
            device_id=(down, parts - 1), device_id_type=MESH)

    def to_up():
        return pltpu.make_async_remote_copy(
            halo_src, halo_left, h_send.at[0], h_recv.at[0],
            device_id=(up, 0), device_id_type=MESH)

    @pl.when(sends_down)
    def _():
        to_down().start()

    @pl.when(sends_up)
    def _():
        to_up().start()

    core = lax.rem(t, 2)
    share = 32 * local
    own_half = pl.ds(pl.multiple_of(core * share, share), share)

    def kern_copy(d):
        return pltpu.make_async_remote_copy(
            kbuf.at[0, own_half, :], kbuf.at[d, own_half, :], k_send.at[d], k_recv.at[d],
            device_id=(t, lax.rem(j + d, parts)), device_id_type=MESH)

    def relay(d):
        return pltpu.make_async_remote_copy(
            kbuf.at[d, own_half, :], kbuf.at[d, own_half, :], r_send.at[d], r_recv.at[d],
            device_id=(t + 1 - 2 * core, j), device_id_type=MESH)

    for d in range(1, parts):
        kern_copy(d).start()

    inten[...] = jnp.zeros_like(inten)

    for load in table_loads:
        load.wait()
    low_lanes = lax.broadcasted_iota(jnp.int32, (2 * FREQ_R, 128), 1) < 64

    def spectra(d):
        kernels = stacked(jnp.concatenate([kbuf[d, 64 * k : 64 * k + 64, :] for k in range(local)], 1))
        by_rows = dot(tap_row[...], kernels)
        for k in range(local):
            place = d * local + k
            taken = by_rows[:, 128 * k : 128 * k + 128]
            high = taken.astype(jnp.bfloat16)
            high_wide = high.astype(jnp.float32)
            low = taken - high_wide
            real = jnp.where(low_lanes, high_wide, pltpu.roll(low, 64, 1)).astype(jnp.bfloat16)
            imag = jnp.where(low_lanes, pltpu.roll(high_wide, 64, 1), low).astype(jnp.bfloat16)
            for part, (own, table) in enumerate(((real, tap_real), (imag, tap_imag))):
                lanes = slice(part * 128, part * 128 + 128)
                pieces = quarters(dot(jnp.concatenate([own, high], 1), table[...]))
                for i, piece in enumerate(pieces):
                    spec[place, i, :, lanes] = piece

    def arrive(d):
        @pl.when(d + 1 < parts)
        def _():
            kern_copy(d + 1).wait_recv()
            relay(d + 1).start()

        relay(d).wait_recv()

    spectra(0)
    kern_copy(1).wait_recv()
    relay(1).start()

    @pl.when(sends_down)
    def _():
        to_down().wait()

    @pl.when(sends_up)
    def _():
        to_up().wait()

    before = jnp.where(first, jnp.where(has_down, halo_left[...], 0.0), mwin[0] * live_rows)
    after = jnp.where(last, jnp.where(has_up, halo_right[...], 0.0), mwin[2] * live_rows)
    window = jnp.concatenate([before[:, SIDE:], here, after[:, :SIDE]], 1)
    by_rows = dot(row_forward[...], stacked(window))
    spectrum = dot3(by_rows, col_hi[...], col_lo[...])
    for place, piece in enumerate(quarters(spectrum)):
        xspec[place] = piece

    def weight_of(d, k):
        return kbuf[d, 64 * k + SUP : 64 * k + SUP + 1, :]

    def field_start(d, k, slot):
        products = []
        for part in range(2):
            lanes = slice(part * 128, part * 128 + 128)
            ur, ui, vr, vi = (spec[d * local + k, i, :, lanes] for i in range(4))
            xur, xui, xvr, xvi = (xspec[i] for i in range(4))
            products.append(
                unquarters(
                    ur * xur - ui * xui, ur * xui + ui * xur,
                    vr * xvr - vi * xvi, vr * xvi + vi * xvr,
                )
            )
        y_hi, y_lo = split(jnp.concatenate(products, 0))
        wide = dot(y_hi, inv_mid[...])
        inner = wide[:, :128] + (wide[:, 128:] + dot(y_lo, inv_mid[:, :128]))
        n = 2 * FREQ_R
        zbuf[slot, k] = stacked(jnp.concatenate([inner[:n], inner[n:]], 1))

    def field_end(d, k, slot):
        field = dot(row_back[...], zbuf[slot, k])
        fields[d * local + k] = field
        real, imag = field[:, :128], field[:, 128:]
        inten[...] += weight_of(d, k) * (real * real + imag * imag)

    def starts(d):
        for k in range(local):
            field_start(d, k, d % 2)

    def ends(d):
        for k in range(local):
            field_end(d, k, d % 2)

    def forward(d, carry):
        arrive(d)
        ends(d - 2)
        starts(d - 1)
        spectra(d)
        return carry

    arrive(1)
    starts(0)
    spectra(1)
    lax.fori_loop(2, parts, forward, 0)
    ends(parts - 2)
    starts(parts - 1)
    ends(parts - 1)

    printed = jax.nn.sigmoid(steepness * (inten[...] - threshold))
    loads[3].wait()
    target = twin[...].astype(jnp.float32)
    inten[...] = live_rows * (4.0 * steepness) * (printed - target) * printed * (1.0 - printed)
    gspec[...] = jnp.zeros_like(gspec)

    def adjoint_start(d, k, slot):
        slope = inten[...] * weight_of(d, k)
        source = fields[d * local + k] * jnp.concatenate([slope, slope], 1)
        by_rows = dot(row_forward[...], stacked(source))
        hi, lo = split(jnp.concatenate([by_rows[:, :128], by_rows[:, 128:]], 0))
        sbuf[slot, k, :, 0:128] = hi
        sbuf[slot, k, :, 128:256] = lo

    def adjoint_end(d, k, slot):
        found = dot(sbuf[slot, k], src_tab[0:256, :]) + dot(sbuf[slot, k, :, 0:128], src_tab[256:384, :])
        n = 2 * FREQ_R
        sums = [0.0] * 4
        for part in range(2):
            lanes = slice(part * 128, part * 128 + 128)
            sur, sui, svr, svi = quarters(found[part * n : part * n + n])
            ur, ui, vr, vi = (spec[d * local + k, i, :, lanes] for i in range(4))
            sums[0] += sur * ur + sui * ui
            sums[1] += sui * ur - sur * ui
            sums[2] += svr * vr + svi * vi
            sums[3] += svi * vr - svr * vi
        for i in range(4):
            gspec[i] += sums[i]

    def adjoint(d, carry):
        for k in range(local):
            adjoint_end(d - 1, k, (d - 1) % 2)
        for k in range(local):
            adjoint_start(d, k, d % 2)
        return carry

    for k in range(local):
        adjoint_start(0, k, 0)
    lax.fori_loop(1, parts, adjoint, 0)
    for k in range(local):
        adjoint_end(parts - 1, k, (parts - 1) % 2)

    total = unquarters(gspec[0], gspec[1], gspec[2], gspec[3])
    inner = dot3(total, inv_hi[...], inv_lo[...])
    gwin[...] = dot(row_back[...], stacked(inner))

    def rows_of(index):
        return pl.ds(pl.multiple_of(index * chunk, chunk), chunk)

    def grad_copy(d):
        other = lax.rem(j + d, parts)
        return pltpu.make_async_remote_copy(
            gwin.at[rows_of(other), :], rbuf.at[d], g_send.at[d], g_recv.at[d],
            device_id=(t, other), device_id_type=MESH)

    def edge_down(i):
        return pltpu.make_async_remote_copy(
            gwin.at[i * chunk : (i + 1) * chunk, 0:128], edge_right, e_send.at[i], e_recv.at[0],
            device_id=(down, i), device_id_type=MESH)

    def edge_up(i):
        return pltpu.make_async_remote_copy(
            gwin.at[i * chunk : (i + 1) * chunk, 128:256], edge_left, e_send.at[i], e_recv.at[1],
            device_id=(up, i), device_id_type=MESH)

    @pl.when(sends_down)
    def _():
        for i in range(parts):
            edge_down(i).start()

    @pl.when(sends_up)
    def _():
        for i in range(parts):
            edge_up(i).start()

    for d in range(1, parts):
        grad_copy(d).start()

    acc[...] = jnp.zeros_like(acc)
    acc[:, pl.ds(pl.multiple_of(j * 128, 128), 256)] += gwin[rows_of(j), :]
    for d in range(1, parts):
        grad_copy(d).wait_recv()
        source = lax.rem(j + parts - d, parts)
        acc[:, pl.ds(pl.multiple_of(source * 128, 128), 256)] += rbuf[d]

    @pl.when(has_up)
    def _():
        edge_down(0).wait_recv()
        acc[:, BLOCK * parts :] += edge_right[...]

    @pl.when(has_down)
    def _():
        edge_up(0).wait_recv()
        acc[:, 0:128] += edge_left[...]

    half_parts = parts // 2
    mine = jnp.where(j < half_parts, flag(0), flag(1))
    out_ref[...] = acc[:, SIDE : SIDE + BLOCK * parts] * mine

    for d in range(1, parts):
        kern_copy(d).wait_send()
        relay(d).wait_send()
        grad_copy(d).wait_send()

    @pl.when(sends_down)
    def _():
        for i in range(parts):
            edge_down(i).wait_send()

    @pl.when(sends_up)
    def _():
        for i in range(parts):
            edge_up(i).wait_send()


def shards(mask_field, target_image, kernels, kernel_weights, live_list, live_count):
    strips, parts = lax.axis_size("tile"), lax.axis_size("kern")
    local = kernels.shape[0]
    count = local * parts
    vmem = pl.BlockSpec(memory_space=pltpu.VMEM)
    smem = pl.BlockSpec(memory_space=pltpu.SMEM)
    hbm = pl.BlockSpec(memory_space=pl.ANY)
    f32 = jnp.float32
    chunk = ROWS // parts
    consts = tables()
    kernels = jnp.transpose(kernels, (0, 2, 1, 3))
    return pl.pallas_call(
        functools.partial(body, strips, parts, local),
        out_shape=jax.ShapeDtypeStruct((chunk, BLOCK * parts), f32),
        in_specs=[hbm, hbm, hbm, smem, smem, smem] + [hbm] * len(consts),
        out_specs=vmem,
        scratch_shapes=[pltpu.VMEM(c.shape, jnp.bfloat16) for c in consts]
        + [
            pltpu.VMEM((2, local, 6 * FREQ_R, 256), jnp.bfloat16),
            pltpu.VMEM((2, local, 4 * FREQ_R, 256), jnp.bfloat16),
            pltpu.VMEM(kernels.shape, f32),
            pltpu.VMEM((3, ROWS, 128), f32),
            pltpu.VMEM((ROWS, 128), jnp.int32),
            pltpu.SemaphoreType.DMA((5,)),
            pltpu.SemaphoreType.DMA((len(consts),)),
            pltpu.VMEM((parts, 64 * local, 128), f32),
            pltpu.VMEM((ROWS, 128), f32),
            pltpu.VMEM((ROWS, 128), f32),
            pltpu.VMEM((ROWS, 128), f32),
            pltpu.VMEM((4, FREQ_R, FREQ_C), f32),
            pltpu.VMEM((count, 4, FREQ_R, 2 * FREQ_C), f32),
            pltpu.VMEM((count, ROWS, 256), f32),
            pltpu.VMEM((ROWS, 128), f32),
            pltpu.VMEM((4, FREQ_R, FREQ_C), f32),
            pltpu.VMEM((ROWS, 256), f32),
            pltpu.VMEM((parts, chunk, 256), f32),
            pltpu.VMEM((chunk, 128), f32),
            pltpu.VMEM((chunk, 128), f32),
            pltpu.VMEM((chunk, BLOCK * parts + 128), f32),
            pltpu.SemaphoreType.DMA((parts,)),
            pltpu.SemaphoreType.DMA((parts,)),
            pltpu.SemaphoreType.DMA((parts,)),
            pltpu.SemaphoreType.DMA((parts,)),
            pltpu.SemaphoreType.DMA((1,)),
            pltpu.SemaphoreType.DMA((1,)),
            pltpu.SemaphoreType.DMA((parts,)),
            pltpu.SemaphoreType.DMA((parts,)),
            pltpu.SemaphoreType.DMA((parts,)),
            pltpu.SemaphoreType.DMA((2,)),
        ],
        compiler_params=pltpu.CompilerParams(
            collective_id=0, has_side_effects=True, vmem_limit_bytes=56 * 1024 * 1024
        ),
    )(mask_field, target_image, kernels, kernel_weights, live_list, live_count, *consts)


def solution(mesh):
    placed = (
        P(None, "tile"),
        P(None, "tile"),
        P("kern", None, None, None),
        P("kern"),
        P("tile", None),
        P("tile"),
    )
    return jax.shard_map(
        shards, mesh=mesh, in_specs=placed, out_specs=P("kern", "tile"), check_vma=False
    )
```

```python
import functools

import jax
import jax.numpy as jnp
import ml_dtypes
import numpy as np
from jax import lax
from jax.experimental import pallas as pl
from jax.experimental.pallas import tpu as pltpu
from jax.sharding import PartitionSpec as P

MESH = pl.DeviceIdType.MESH
steepness = 4.0
threshold = 0.6

ROWS = 128
BLOCK = 128
RIM = 30
SUP = 61
PERIOD_R = 159
FREQ_R = 80
PERIOD_C = 255
FREQ_C = 128
SIDE = 64


def split_np(table):
    hi = table.astype(np.float32).astype(ml_dtypes.bfloat16)
    lo = (table - hi.astype(np.float64)).astype(np.float32).astype(ml_dtypes.bfloat16)
    return hi, lo


def phases(first, second, period):
    angle = 2.0 * np.pi / period * (np.outer(first, second) % period)
    return np.cos(angle), np.sin(angle)


@functools.cache
def tables():
    fr, fc = np.arange(FREQ_R), np.arange(FREQ_C)
    rows, window = np.arange(ROWS), np.arange(2 * BLOCK)
    taps = np.arange(SUP) - RIM
    row_weight = np.where(fr == 0, 1.0, 2.0) / PERIOD_R
    col_weight = np.where(fc == 0, 1.0, 2.0) / PERIOD_C * 0.5
    c, s = phases(fr, rows, PERIOD_R)
    to_rows_hi, to_rows_lo = split_np(np.concatenate([c, s], 0))
    row_forward = np.concatenate([to_rows_hi, to_rows_hi, to_rows_lo], 1)
    back = np.concatenate([c * row_weight[:, None], s * row_weight[:, None]], 0).T
    back_hi, back_lo = split_np(back)
    row_back = np.concatenate([back_hi, back_hi, back_lo], 1)
    c, s = phases(window, fc, PERIOD_C)
    col_hi, col_lo = split_np(np.concatenate([c, s], 1))
    inv = np.concatenate([(c * col_weight).T, (s * col_weight).T], 0)
    inv_hi, inv_lo = split_np(inv)
    mid = slice(SIDE, SIDE + BLOCK)
    inv_mid = np.concatenate([inv_hi[:, mid], inv_lo[:, mid]], 1)
    src_hi = np.concatenate([col_hi[mid], col_hi[mid], col_lo[mid]], 0)
    c, s = phases(taps, fc, PERIOD_C)
    tap_cols = np.zeros((64, 2 * FREQ_C))
    tap_cols[:SUP] = np.concatenate([c, s], 1)
    tc_hi, tc_lo = split_np(tap_cols)
    zero = np.zeros_like(tc_hi)
    tap_real = np.concatenate([tc_hi, tc_hi, tc_lo, zero], 0)
    tap_imag = np.concatenate([tc_hi, tc_hi, zero, tc_lo], 0)
    c, s = phases(fr, taps, PERIOD_R)
    tap_rows = np.zeros((2 * FREQ_R, 64))
    tap_rows[:, :SUP] = np.concatenate([c, s], 0)
    tr_hi, tr_lo = split_np(tap_rows)
    tap_row = np.concatenate([tr_hi, tr_hi, tr_lo], 1)
    return (row_forward, row_back, col_hi, col_lo, inv_hi, inv_lo, inv_mid, src_hi, tap_real, tap_imag, tap_row)


def split(value):
    hi = value.astype(jnp.bfloat16)
    lo = (value - hi.astype(jnp.float32)).astype(jnp.bfloat16)
    return hi, lo


def dot(a, b):
    return jnp.dot(a, b, preferred_element_type=jnp.float32)


def dot3(a, b_hi, b_lo):
    a_hi, a_lo = split(a)
    return dot(a_hi, b_hi) + (dot(a_lo, b_hi) + dot(a_hi, b_lo))


def stacked(value):
    hi, lo = split(value)
    return jnp.concatenate([hi, lo, hi], 0)


def quarters(spec):
    cc, cs = spec[:FREQ_R, :FREQ_C], spec[:FREQ_R, FREQ_C:]
    sc, ss = spec[FREQ_R:, :FREQ_C], spec[FREQ_R:, FREQ_C:]
    return cc - ss, cs + sc, cc + ss, sc - cs


def unquarters(ur, ui, vr, vi):
    top = jnp.concatenate([ur + vr, ui - vi], 1)
    bottom = jnp.concatenate([ui + vi, vr - ur], 1)
    return jnp.concatenate([top, bottom], 0)


def body(
    strips, parts, local,
    mask_ref, target_ref, kern_ref, weight_ref, list_ref, count_ref, *rest,
):
    table_count = len(tables())
    in_hbm, rest = rest[:table_count], rest[table_count:]
    out_ref, rest = rest[0], rest[1:]
    held, rest = rest[:table_count], rest[table_count:]
    run(strips, parts, local, mask_ref, target_ref, kern_ref, weight_ref, list_ref, count_ref, in_hbm, out_ref, held, *rest)


def run(
    strips, parts, local,
    mask_ref, target_ref, kern_ref, weight_ref, list_ref, count_ref, in_hbm, out_ref, held,
    zbuf, sbuf, raw, mwin, twin, l_sem, t_sem,
    kbuf, halo_src, halo_left, halo_right, xspec, spec, fields, inten, other, slope, gspec, gwin, rbuf,
    edge_left, edge_right, acc,
    ready, k_send, k_recv, h_send, h_recv, p_send, p_recv, g_send, g_recv, e_send, e_recv,
):
    t = lax.axis_index("tile")
    j = lax.axis_index("kern")
    up = lax.rem(t + 1, strips)
    down = lax.rem(t + strips - 1, strips)
    chunk = ROWS // parts
    groups = parts // 2

    def columns_of(device):
        return 2 * lax.rem((device // 2 + 1) // 2, 2) + lax.rem(device, 2)

    def device_of(half, columns):
        inner = columns // 2
        return 2 * (inner + half * (3 - 2 * inner)) + lax.rem(columns, 2)

    mine_half, x = j // 4, columns_of(j)
    first, last = x == 0, x == groups - 1
    has_up, has_down = t < strips - 1, t > 0
    sends_up, sends_down = last & has_up, first & has_down
    left_end, right_end = device_of(mine_half, 0), device_of(mine_half, groups - 1)
    row_forward, row_back, col_hi, col_lo, inv_hi, inv_lo, inv_mid, src_tab, tap_real, tap_imag, tap_row = held

    def strip_column(ref, index):
        return ref.at[:, pl.ds(pl.multiple_of(index * 128, 128), 128)]

    def block_at(group, turn):
        return jnp.where(group == 0, 1 - turn, turn)

    kern_load = pltpu.make_async_copy(kern_ref, raw, l_sem.at[0])
    kern_load.start()
    at = 2 * x
    places = (jnp.maximum(at - 1, 0), at, at + 1, jnp.minimum(at + 2, parts - 1))
    loads = [
        pltpu.make_async_copy(strip_column(mask_ref, place), mwin.at[i], l_sem.at[1 + i])
        for i, place in enumerate(places)
    ]
    target_loads = [
        pltpu.make_async_copy(strip_column(target_ref, at + block_at(x, b)), twin.at[b], l_sem.at[5 + b])
        for b in range(2)
    ]
    table_loads = [
        pltpu.make_async_copy(source, place, t_sem.at[i]) for i, (source, place) in enumerate(zip(in_hbm, held))
    ]
    for load in loads + table_loads + target_loads:
        load.start()

    barrier = pltpu.get_barrier_semaphore()
    for d in range(1, parts):
        pl.semaphore_signal(barrier, inc=1, device_id=(t, lax.rem(j + d, parts)), device_id_type=MESH)

    @pl.when(sends_up)
    def _():
        pl.semaphore_signal(barrier, inc=1, device_id=(up, left_end), device_id_type=MESH)

    @pl.when(sends_down)
    def _():
        pl.semaphore_signal(barrier, inc=1, device_id=(down, right_end), device_id_type=MESH)

    kbuf[0] = jnp.zeros_like(kbuf[0])
    kern_load.wait()
    for k in range(local):
        kbuf[0, 64 * k : 64 * k + SUP, 0:SUP] = raw[k, :, 0, :]
        kbuf[0, 64 * k : 64 * k + SUP, 64 : 64 + SUP] = raw[k, :, 1, :]
        kbuf[0, 64 * k + SUP : 64 * k + SUP + 1, :] = jnp.full((1, 128), weight_ref[k], jnp.float32)

    def flag(slot):
        found = jnp.float32(0.0)
        for place in range(2):
            hit = (list_ref[0, place] == slot) & (place < count_ref[0])
            found = jnp.where(hit, jnp.float32(1.0), found)
        return found

    half = ROWS // 2
    live_rows = jnp.concatenate(
        [jnp.full((half, 128), flag(0), jnp.float32), jnp.full((half, 128), flag(1), jnp.float32)], 0
    )

    for load in loads:
        load.wait()
    halo_src[...] = jnp.where(first, mwin[1], mwin[2]) * live_rows

    edge_device = sends_up | sends_down

    @pl.when(edge_device)
    def _():
        pl.semaphore_wait(barrier, parts)

    @pl.when(jnp.logical_not(edge_device))
    def _():
        pl.semaphore_wait(barrier, parts - 1)

    def to_down():
        return pltpu.make_async_remote_copy(
            halo_src, halo_right, h_send.at[0], h_recv.at[0],
            device_id=(down, right_end), device_id_type=MESH)

    def to_up():
        return pltpu.make_async_remote_copy(
            halo_src, halo_left, h_send.at[0], h_recv.at[0],
            device_id=(up, left_end), device_id_type=MESH)

    @pl.when(sends_down)
    def _():
        to_down().start()
        pl.semaphore_signal(ready, inc=1, device_id=(down, right_end), device_id_type=MESH)

    @pl.when(sends_up)
    def _():
        to_up().start()
        pl.semaphore_signal(ready, inc=1, device_id=(up, left_end), device_id_type=MESH)

    x_hi, x_lo = x // 2, lax.rem(x, 2)
    peers = [x, 2 * (1 - x_hi) + x_lo, 2 * x_hi + 1 - x_lo, 2 * (1 - x_hi) + 1 - x_lo]

    def kern_copy(slot, peer=peers[1]):
        return pltpu.make_async_remote_copy(
            kbuf.at[0], kbuf.at[slot], k_send.at[slot], k_recv.at[slot],
            device_id=(t, device_of(mine_half, peer)), device_id_type=MESH)

    for slot in range(1, groups):
        kern_copy(slot, peers[slot]).start()

    for load in table_loads:
        load.wait()
    low_lanes = lax.broadcasted_iota(jnp.int32, (2 * FREQ_R, 128), 1) < 64

    def spectra(e):
        kernels = stacked(jnp.concatenate([kbuf[e, 64 * k : 64 * k + 64, :] for k in range(local)], 1))
        by_rows = dot(tap_row[...], kernels)
        for k in range(local):
            place = e * local + k
            taken = by_rows[:, 128 * k : 128 * k + 128]
            high = taken.astype(jnp.bfloat16)
            high_wide = high.astype(jnp.float32)
            low = taken - high_wide
            real = jnp.where(low_lanes, high_wide, pltpu.roll(low, 64, 1)).astype(jnp.bfloat16)
            imag = jnp.where(low_lanes, pltpu.roll(high_wide, 64, 1), low).astype(jnp.bfloat16)
            for part, (own, table) in enumerate(((real, tap_real), (imag, tap_imag))):
                lanes = slice(part * 128, part * 128 + 128)
                pieces = quarters(dot(jnp.concatenate([own, high], 1), table[...]))
                for i, piece in enumerate(pieces):
                    spec[place, i, :, lanes] = piece

    def weight_of(e, k):
        return kbuf[e, 64 * k + SUP : 64 * k + SUP + 1, :]

    def starts(e, b):
        n = 2 * FREQ_R
        for k in range(local):
            products = []
            for part in range(2):
                lanes = slice(part * 128, part * 128 + 128)
                ur, ui, vr, vi = (spec[e * local + k, i, :, lanes] for i in range(4))
                xur, xui, xvr, xvi = (xspec[b, i] for i in range(4))
                products.append(
                    unquarters(
                        ur * xur - ui * xui, ur * xui + ui * xur,
                        vr * xvr - vi * xvi, vr * xvi + vi * xvr,
                    )
                )
            y_hi, y_lo = split(jnp.concatenate(products, 0))
            wide = dot(y_hi, inv_mid[...])
            inner = wide[:, :128] + (wide[:, 128:] + dot(y_lo, inv_mid[:, :128]))
            zbuf[b, k] = stacked(jnp.concatenate([inner[:n], inner[n:]], 1))

    def ends(e, b):
        for k in range(local):
            field = dot(row_back[...], zbuf[b, k])
            fields[b, e * local + k] = field
            real, imag = field[:, :128], field[:, 128:]
            inten[b] += weight_of(e, k) * (real * real + imag * imag)

    spectra(0)

    pair = [mwin[1] * live_rows, mwin[2] * live_rows]

    def transform(b, window):
        by_rows = dot(row_forward[...], stacked(window))
        spectrum = dot3(by_rows, col_hi[...], col_lo[...])
        for i, piece in enumerate(quarters(spectrum)):
            xspec[b, i] = piece

    before, after = mwin[0] * live_rows, mwin[3] * live_rows
    left = jnp.concatenate([before[:, SIDE:], pair[0], pair[1][:, :SIDE]], 1)
    right = jnp.concatenate([pair[0][:, SIDE:], pair[1], after[:, :SIDE]], 1)
    transform(0, jnp.where(first, right, left))
    inten[...] = jnp.zeros_like(inten)

    def forward(e, carry):
        ends(e - 1, 0)
        kern_copy(e).wait_recv()
        spectra(e)
        starts(e, 0)
        return carry

    def second(e, carry):
        ends(e - 1, 1)
        starts(e, 1)
        return carry

    def swap(b):
        return pltpu.make_async_remote_copy(
            inten.at[b], other.at[b], p_send.at[b], p_recv.at[b],
            device_id=(t, device_of(1 - mine_half, x)), device_id_type=MESH)

    starts(0, 0)
    lax.fori_loop(1, groups, forward, 0)
    ends(groups - 1, 0)
    swap(0).start()

    @pl.when(sends_down)
    def _():
        to_down().wait()

    @pl.when(sends_up)
    def _():
        to_up().wait()

    before = jnp.where(has_down, halo_left[...], 0.0)
    after = jnp.where(last, jnp.where(has_up, halo_right[...], 0.0), mwin[3] * live_rows)
    left = jnp.concatenate([before[:, SIDE:], pair[0], pair[1][:, :SIDE]], 1)
    right = jnp.concatenate([pair[0][:, SIDE:], pair[1], after[:, :SIDE]], 1)
    transform(1, jnp.where(first, left, right))
    starts(0, 1)
    lax.fori_loop(1, groups, second, 0)
    ends(groups - 1, 1)
    swap(1).start()
    gspec[...] = jnp.zeros_like(gspec)

    def slope_of(b):
        target_loads[b].wait()
        swap(b).wait_recv()
        printed = jax.nn.sigmoid(steepness * (inten[b] + other[b] - threshold))
        target = twin[b].astype(jnp.float32)
        slope[b] = live_rows * (4.0 * steepness) * (printed - target) * printed * (1.0 - printed)

    def adjoint_start(e, b, slot):
        for k in range(local):
            tilt = slope[b] * weight_of(e, k)
            source = fields[b, e * local + k] * jnp.concatenate([tilt, tilt], 1)
            by_rows = dot(row_forward[...], stacked(source))
            hi, lo = split(jnp.concatenate([by_rows[:, :128], by_rows[:, 128:]], 0))
            sbuf[slot, k, :, 0:128] = hi
            sbuf[slot, k, :, 128:256] = lo

    def adjoint_end(e, b, slot):
        n = 2 * FREQ_R
        for k in range(local):
            found = dot(sbuf[slot, k], src_tab[0:256, :]) + dot(sbuf[slot, k, :, 0:128], src_tab[256:384, :])
            sums = [0.0] * 4
            for part in range(2):
                lanes = slice(part * 128, part * 128 + 128)
                sur, sui, svr, svi = quarters(found[part * n : part * n + n])
                ur, ui, vr, vi = (spec[e * local + k, i, :, lanes] for i in range(4))
                sums[0] += sur * ur + sui * ui
                sums[1] += sui * ur - sur * ui
                sums[2] += svr * vr + svi * vi
                sums[3] += svi * vr - svr * vi
            for i in range(4):
                gspec[b, i] += sums[i]

    def adjoint(b):
        def step(e, carry):
            adjoint_end(e - 1, b, (e - 1) % 2)
            adjoint_start(e, b, e % 2)
            return carry

        return step

    def inverse(b):
        total = unquarters(gspec[b, 0], gspec[b, 1], gspec[b, 2], gspec[b, 3])
        gwin[b] = dot(row_back[...], stacked(dot3(total, inv_hi[...], inv_lo[...])))

    def rows_of(index):
        return pl.ds(pl.multiple_of(index * chunk, chunk), chunk)

    def grad_copy(b, d):
        owner = lax.rem(j + d, parts)
        return pltpu.make_async_remote_copy(
            gwin.at[b, rows_of(owner), :], rbuf.at[b, d], g_send.at[b, d], g_recv.at[b, d],
            device_id=(t, owner), device_id_type=MESH)

    def edge_down(i):
        return pltpu.make_async_remote_copy(
            gwin.at[1, i * chunk : (i + 1) * chunk, 0:128], edge_right.at[mine_half], e_send.at[i], e_recv.at[0, mine_half],
            device_id=(down, i), device_id_type=MESH)

    def edge_up(i):
        return pltpu.make_async_remote_copy(
            gwin.at[1, i * chunk : (i + 1) * chunk, 128:256], edge_left.at[mine_half], e_send.at[i], e_recv.at[1, mine_half],
            device_id=(up, i), device_id_type=MESH)

    end = groups - 1
    slope_of(0)
    adjoint_start(0, 0, 0)
    lax.fori_loop(1, groups, adjoint(0), 0)
    slope_of(1)
    adjoint_end(end, 0, end % 2)
    adjoint_start(0, 1, 0)
    inverse(0)

    for d in range(1, parts):
        grad_copy(0, d).start()
    lax.fori_loop(1, groups, adjoint(1), 0)
    adjoint_end(end, 1, end % 2)
    inverse(1)

    @pl.when(sends_down)
    def _():
        pl.semaphore_wait(ready, 1)
        for i in range(parts):
            edge_down(i).start()

    @pl.when(sends_up)
    def _():
        pl.semaphore_wait(ready, 1)
        for i in range(parts):
            edge_up(i).start()

    for d in range(1, parts):
        grad_copy(1, d).start()

    def span(source, b):
        group = columns_of(source)
        return pl.ds(pl.multiple_of((2 * group + block_at(group, b)) * 128, 128), 256)

    acc[...] = jnp.zeros_like(acc)
    for b in range(2):
        acc[:, span(j, b)] += gwin[b, rows_of(j), :]
        for d in range(1, parts):
            grad_copy(b, d).wait_recv()
            acc[:, span(lax.rem(j + parts - d, parts), b)] += rbuf[b, d]

    @pl.when(has_up)
    def _():
        for side in range(2):
            pltpu.make_async_copy(edge_right.at[side], edge_right.at[side], e_recv.at[0, side]).wait()
        acc[:, BLOCK * parts :] += edge_right[0] + edge_right[1]

    @pl.when(has_down)
    def _():
        for side in range(2):
            pltpu.make_async_copy(edge_left.at[side], edge_left.at[side], e_recv.at[1, side]).wait()
        acc[:, 0:128] += edge_left[0] + edge_left[1]

    mine = jnp.where(j < groups, flag(0), flag(1))
    out_ref[...] = acc[:, SIDE : SIDE + BLOCK * parts] * mine

    for slot in range(1, groups):
        kern_copy(slot).wait_send()
    for b in range(2):
        swap(b).wait_send()
        for d in range(1, parts):
            grad_copy(b, d).wait_send()

    @pl.when(sends_down)
    def _():
        for i in range(parts):
            edge_down(i).wait_send()

    @pl.when(sends_up)
    def _():
        for i in range(parts):
            edge_up(i).wait_send()


def shards(mask_field, target_image, kernels, kernel_weights, live_list, live_count):
    strips, parts = lax.axis_size("tile"), lax.axis_size("kern")
    local = kernels.shape[0]
    groups = parts // 2
    count = local * groups
    vmem = pl.BlockSpec(memory_space=pltpu.VMEM)
    smem = pl.BlockSpec(memory_space=pltpu.SMEM)
    hbm = pl.BlockSpec(memory_space=pl.ANY)
    f32, bf16 = jnp.float32, jnp.bfloat16
    dma = pltpu.SemaphoreType.DMA
    chunk = ROWS // parts
    consts = tables()
    kernels = jnp.transpose(kernels, (0, 2, 1, 3))
    return pl.pallas_call(
        functools.partial(body, strips, parts, local),
        out_shape=jax.ShapeDtypeStruct((chunk, BLOCK * parts), f32),
        in_specs=[hbm, hbm, hbm, smem, smem, smem] + [hbm] * len(consts),
        out_specs=vmem,
        scratch_shapes=[pltpu.VMEM(c.shape, bf16) for c in consts]
        + [
            pltpu.VMEM((2, local, 6 * FREQ_R, 256), bf16),
            pltpu.VMEM((2, local, 4 * FREQ_R, 256), bf16),
            pltpu.VMEM(kernels.shape, f32),
            pltpu.VMEM((4, ROWS, 128), f32),
            pltpu.VMEM((2, ROWS, 128), jnp.int32),
            dma((7,)),
            dma((len(consts),)),
            pltpu.VMEM((groups, 64 * local, 128), f32),
            pltpu.VMEM((ROWS, 128), f32),
            pltpu.VMEM((ROWS, 128), f32),
            pltpu.VMEM((ROWS, 128), f32),
            pltpu.VMEM((2, 4, FREQ_R, FREQ_C), f32),
            pltpu.VMEM((count, 4, FREQ_R, 2 * FREQ_C), f32),
            pltpu.VMEM((2, count, ROWS, 256), f32),
            pltpu.VMEM((2, ROWS, 128), f32),
            pltpu.VMEM((2, ROWS, 128), f32),
            pltpu.VMEM((2, ROWS, 128), f32),
            pltpu.VMEM((2, 4, FREQ_R, FREQ_C), f32),
            pltpu.VMEM((2, ROWS, 256), f32),
            pltpu.VMEM((2, parts, chunk, 256), f32),
            pltpu.VMEM((2, chunk, 128), f32),
            pltpu.VMEM((2, chunk, 128), f32),
            pltpu.VMEM((chunk, BLOCK * parts + 128), f32),
            pltpu.SemaphoreType.REGULAR,
            dma((groups,)),
            dma((groups,)),
            dma((1,)),
            dma((1,)),
            dma((2,)),
            dma((2,)),
            dma((2, parts)),
            dma((2, parts)),
            dma((parts,)),
            dma((2, 2)),
        ],
        compiler_params=pltpu.CompilerParams(
            collective_id=0, has_side_effects=True, vmem_limit_bytes=56 * 1024 * 1024
        ),
    )(mask_field, target_image, kernels, kernel_weights, live_list, live_count, *consts)


def solution(mesh):
    placed = (
        P(None, "tile"),
        P(None, "tile"),
        P("kern", None, None, None),
        P("kern"),
        P("tile", None),
        P("tile"),
    )
    return jax.shard_map(
        shards, mesh=mesh, in_specs=placed, out_specs=P("kern", "tile"), check_vma=False
    )
```

```python
import functools

import jax
import jax.numpy as jnp
import ml_dtypes
import numpy as np
from jax import lax
from jax.experimental import pallas as pl
from jax.experimental.pallas import tpu as pltpu
from jax.sharding import PartitionSpec as P

MESH = pl.DeviceIdType.MESH
steepness = 4.0
threshold = 0.6

ROWS = 128
BLOCK = 128
RIM = 30
SUP = 61
PERIOD_R = 159
FREQ_R = 80
PERIOD_C = 255
FREQ_C = 128
SIDE = 64


def split_np(table):
    hi = table.astype(np.float32).astype(ml_dtypes.bfloat16)
    lo = (table - hi.astype(np.float64)).astype(np.float32).astype(ml_dtypes.bfloat16)
    return hi, lo


def phases(first, second, period):
    angle = 2.0 * np.pi / period * (np.outer(first, second) % period)
    return np.cos(angle), np.sin(angle)


@functools.cache
def tables():
    fr, fc = np.arange(FREQ_R), np.arange(FREQ_C)
    rows, window = np.arange(ROWS), np.arange(2 * BLOCK)
    taps = np.arange(SUP) - RIM
    row_weight = np.where(fr == 0, 1.0, 2.0) / PERIOD_R
    col_weight = np.where(fc == 0, 1.0, 2.0) / PERIOD_C * 0.5
    c, s = phases(fr, rows, PERIOD_R)
    to_rows_hi, to_rows_lo = split_np(np.concatenate([c, s], 0))
    row_forward = np.concatenate([to_rows_hi, to_rows_hi, to_rows_lo], 1)
    back = np.concatenate([c * row_weight[:, None], s * row_weight[:, None]], 0).T
    back_hi, back_lo = split_np(back)
    row_back = np.concatenate([back_hi, back_hi, back_lo], 1)
    c, s = phases(window, fc, PERIOD_C)
    col_hi, col_lo = split_np(np.concatenate([c, s], 1))
    inv = np.concatenate([(c * col_weight).T, (s * col_weight).T], 0)
    inv_hi, inv_lo = split_np(inv)
    mid = slice(SIDE, SIDE + BLOCK)
    inv_mid = np.concatenate([inv_hi[:, mid], inv_lo[:, mid]], 1)
    src_hi = np.concatenate([col_hi[mid], col_hi[mid], col_lo[mid]], 0)
    c, s = phases(taps, fc, PERIOD_C)
    tap_cols = np.zeros((64, 2 * FREQ_C))
    tap_cols[:SUP] = np.concatenate([c, s], 1)
    tc_hi, tc_lo = split_np(tap_cols)
    zero = np.zeros_like(tc_hi)
    tap_real = np.concatenate([tc_hi, tc_hi, tc_lo, zero], 0)
    tap_imag = np.concatenate([tc_hi, tc_hi, zero, tc_lo], 0)
    c, s = phases(fr, taps, PERIOD_R)
    tap_rows = np.zeros((2 * FREQ_R, 64))
    tap_rows[:, :SUP] = np.concatenate([c, s], 0)
    tr_hi, tr_lo = split_np(tap_rows)
    tap_row = np.concatenate([tr_hi, tr_hi, tr_lo], 1)
    return (row_forward, row_back, col_hi, col_lo, inv_hi, inv_lo, inv_mid, src_hi, tap_real, tap_imag, tap_row)


def split(value):
    hi = value.astype(jnp.bfloat16)
    lo = (value - hi.astype(jnp.float32)).astype(jnp.bfloat16)
    return hi, lo


def dot(a, b):
    return jnp.dot(a, b, preferred_element_type=jnp.float32)


def dot3(a, b_hi, b_lo):
    a_hi, a_lo = split(a)
    return dot(a_hi, b_hi) + (dot(a_lo, b_hi) + dot(a_hi, b_lo))


def stacked(value):
    hi, lo = split(value)
    return jnp.concatenate([hi, lo, hi], 0)


def quarters(spec):
    cc, cs = spec[:FREQ_R, :FREQ_C], spec[:FREQ_R, FREQ_C:]
    sc, ss = spec[FREQ_R:, :FREQ_C], spec[FREQ_R:, FREQ_C:]
    return cc - ss, cs + sc, cc + ss, sc - cs


def unquarters(ur, ui, vr, vi):
    top = jnp.concatenate([ur + vr, ui - vi], 1)
    bottom = jnp.concatenate([ui + vi, vr - ur], 1)
    return jnp.concatenate([top, bottom], 0)


def body(
    strips, parts, local,
    mask_ref, target_ref, kern_ref, weight_ref, list_ref, count_ref, *rest,
):
    table_count = len(tables())
    in_hbm, rest = rest[:table_count], rest[table_count:]
    out_ref, rest = rest[0], rest[1:]
    held, rest = rest[:table_count], rest[table_count:]
    run(strips, parts, local, mask_ref, target_ref, kern_ref, weight_ref, list_ref, count_ref, in_hbm, out_ref, held, *rest)


def run(
    strips, parts, local,
    mask_ref, target_ref, kern_ref, weight_ref, list_ref, count_ref, in_hbm, out_ref, held,
    zbuf, sbuf, raw, mwin, twin, l_sem, t_sem,
    kbuf, halo_src, halo_left, halo_right, xspec, spec, fields, inten, other, slope, gspec, gwin, rbuf,
    edge_left, edge_right, acc,
    ready, k_send, k_recv, h_send, h_recv, p_send, p_recv, g_send, g_recv, e_send, e_recv,
):
    t = lax.axis_index("tile")
    j = lax.axis_index("kern")
    up = lax.rem(t + 1, strips)
    down = lax.rem(t + strips - 1, strips)
    chunk = ROWS // parts
    groups = parts // 2

    def columns_of(device):
        return 2 * lax.rem((device // 2 + 1) // 2, 2) + lax.rem(device, 2)

    def device_of(half, columns):
        inner = columns // 2
        return 2 * (inner + half * (3 - 2 * inner)) + lax.rem(columns, 2)

    mine_half, x = j // 4, columns_of(j)
    first, last = x == 0, x == groups - 1
    has_up, has_down = t < strips - 1, t > 0
    sends_up, sends_down = last & has_up, first & has_down
    left_end, right_end = device_of(mine_half, 0), device_of(mine_half, groups - 1)
    row_forward, row_back, col_hi, col_lo, inv_hi, inv_lo, inv_mid, src_tab, tap_real, tap_imag, tap_row = held

    def strip_column(ref, index):
        return ref.at[:, pl.ds(pl.multiple_of(index * 128, 128), 128)]

    def block_at(group, turn):
        return jnp.where(group == 0, 1 - turn, turn)

    kern_load = pltpu.make_async_copy(kern_ref, raw, l_sem.at[0])
    kern_load.start()

    x_hi, x_lo = x // 2, lax.rem(x, 2)
    peers = [x, 2 * (1 - x_hi) + x_lo, 2 * x_hi + 1 - x_lo, 2 * (1 - x_hi) + 1 - x_lo]

    barrier = pltpu.get_barrier_semaphore()
    greeted = [device_of(mine_half, peer) for peer in peers[1:]] + [device_of(1 - mine_half, x)]
    for device in greeted:
        pl.semaphore_signal(barrier, inc=1, device_id=(t, device), device_id_type=MESH)

    @pl.when(sends_up)
    def _():
        pl.semaphore_signal(barrier, inc=1, device_id=(up, left_end), device_id_type=MESH)

    @pl.when(sends_down)
    def _():
        pl.semaphore_signal(barrier, inc=1, device_id=(down, right_end), device_id_type=MESH)

    at = 2 * x
    places = (jnp.maximum(at - 1, 0), at, at + 1, jnp.minimum(at + 2, parts - 1))
    loads = [
        pltpu.make_async_copy(strip_column(mask_ref, place), mwin.at[i], l_sem.at[1 + i])
        for i, place in enumerate(places)
    ]
    target_loads = [
        pltpu.make_async_copy(strip_column(target_ref, at + block_at(x, b)), twin.at[b], l_sem.at[5 + b])
        for b in range(2)
    ]
    table_loads = [
        pltpu.make_async_copy(source, place, t_sem.at[i]) for i, (source, place) in enumerate(zip(in_hbm, held))
    ]
    for load in loads + table_loads + target_loads:
        load.start()

    kbuf[0] = jnp.zeros_like(kbuf[0])
    kern_load.wait()
    for k in range(local):
        kbuf[0, 64 * k : 64 * k + SUP, 0:SUP] = raw[k, :, 0, :]
        kbuf[0, 64 * k : 64 * k + SUP, 64 : 64 + SUP] = raw[k, :, 1, :]
        kbuf[0, 64 * k + SUP : 64 * k + SUP + 1, :] = jnp.full((1, 128), weight_ref[k], jnp.float32)

    def flag(slot):
        found = jnp.float32(0.0)
        for place in range(2):
            hit = (list_ref[0, place] == slot) & (place < count_ref[0])
            found = jnp.where(hit, jnp.float32(1.0), found)
        return found

    half = ROWS // 2
    live_rows = jnp.concatenate(
        [jnp.full((half, 128), flag(0), jnp.float32), jnp.full((half, 128), flag(1), jnp.float32)], 0
    )

    edge_device = sends_up | sends_down

    @pl.when(edge_device)
    def _():
        pl.semaphore_wait(barrier, len(greeted) + 1)

    @pl.when(jnp.logical_not(edge_device))
    def _():
        pl.semaphore_wait(barrier, len(greeted))

    def to_down():
        return pltpu.make_async_remote_copy(
            halo_src, halo_right, h_send.at[0], h_recv.at[0],
            device_id=(down, right_end), device_id_type=MESH)

    def to_up():
        return pltpu.make_async_remote_copy(
            halo_src, halo_left, h_send.at[0], h_recv.at[0],
            device_id=(up, left_end), device_id_type=MESH)

    def kern_copy(slot, peer=peers[1]):
        return pltpu.make_async_remote_copy(
            kbuf.at[0], kbuf.at[slot], k_send.at[slot], k_recv.at[slot],
            device_id=(t, device_of(mine_half, peer)), device_id_type=MESH)

    for slot in range(1, groups):
        kern_copy(slot, peers[slot]).start()

    for load in loads:
        load.wait()
    halo_src[...] = jnp.where(first, mwin[1], mwin[2]) * live_rows

    @pl.when(sends_down)
    def _():
        to_down().start()

    @pl.when(sends_up)
    def _():
        to_up().start()

    for load in table_loads:
        load.wait()
    low_lanes = lax.broadcasted_iota(jnp.int32, (2 * FREQ_R, 128), 1) < 64

    def spectra(e):
        kernels = stacked(jnp.concatenate([kbuf[e, 64 * k : 64 * k + 64, :] for k in range(local)], 1))
        by_rows = dot(tap_row[...], kernels)
        for k in range(local):
            place = e * local + k
            taken = by_rows[:, 128 * k : 128 * k + 128]
            high = taken.astype(jnp.bfloat16)
            high_wide = high.astype(jnp.float32)
            low = taken - high_wide
            real = jnp.where(low_lanes, high_wide, pltpu.roll(low, 64, 1)).astype(jnp.bfloat16)
            imag = jnp.where(low_lanes, pltpu.roll(high_wide, 64, 1), low).astype(jnp.bfloat16)
            for part, (own, table) in enumerate(((real, tap_real), (imag, tap_imag))):
                lanes = slice(part * 128, part * 128 + 128)
                pieces = quarters(dot(jnp.concatenate([own, high], 1), table[...]))
                for i, piece in enumerate(pieces):
                    spec[place, i, :, lanes] = piece

    def weight_of(e, k):
        return kbuf[e, 64 * k + SUP : 64 * k + SUP + 1, :]

    def starts(e, b):
        n = 2 * FREQ_R
        for k in range(local):
            products = []
            for part in range(2):
                lanes = slice(part * 128, part * 128 + 128)
                ur, ui, vr, vi = (spec[e * local + k, i, :, lanes] for i in range(4))
                xur, xui, xvr, xvi = (xspec[b, i] for i in range(4))
                products.append(
                    unquarters(
                        ur * xur - ui * xui, ur * xui + ui * xur,
                        vr * xvr - vi * xvi, vr * xvi + vi * xvr,
                    )
                )
            y_hi, y_lo = split(jnp.concatenate(products, 0))
            wide = dot(y_hi, inv_mid[...])
            inner = wide[:, :128] + (wide[:, 128:] + dot(y_lo, inv_mid[:, :128]))
            zbuf[b, k] = stacked(jnp.concatenate([inner[:n], inner[n:]], 1))

    def ends(e, b):
        for k in range(local):
            field = dot(row_back[...], zbuf[b, k])
            fields[b, e * local + k] = field
            real, imag = field[:, :128], field[:, 128:]
            inten[b] += weight_of(e, k) * (real * real + imag * imag)

    spectra(0)

    pair = [mwin[1] * live_rows, mwin[2] * live_rows]

    def transform(b, window):
        by_rows = dot(row_forward[...], stacked(window))
        spectrum = dot3(by_rows, col_hi[...], col_lo[...])
        for i, piece in enumerate(quarters(spectrum)):
            xspec[b, i] = piece

    before, after = mwin[0] * live_rows, mwin[3] * live_rows
    left = jnp.concatenate([before[:, SIDE:], pair[0], pair[1][:, :SIDE]], 1)
    right = jnp.concatenate([pair[0][:, SIDE:], pair[1], after[:, :SIDE]], 1)
    transform(0, jnp.where(first, right, left))
    inten[...] = jnp.zeros_like(inten)

    def forward(e, carry):
        ends(e - 1, 0)
        kern_copy(e).wait_recv()
        spectra(e)
        starts(e, 0)
        return carry

    def second(e, carry):
        ends(e - 1, 1)
        starts(e, 1)
        return carry

    def swap(b):
        return pltpu.make_async_remote_copy(
            inten.at[b], other.at[b], p_send.at[b], p_recv.at[b],
            device_id=(t, device_of(1 - mine_half, x)), device_id_type=MESH)

    starts(0, 0)
    lax.fori_loop(1, groups, forward, 0)
    ends(groups - 1, 0)
    swap(0).start()

    @pl.when(sends_down)
    def _():
        to_down().wait()

    @pl.when(sends_up)
    def _():
        to_up().wait()

    before = jnp.where(has_down, halo_left[...], 0.0)
    after = jnp.where(last, jnp.where(has_up, halo_right[...], 0.0), mwin[3] * live_rows)
    left = jnp.concatenate([before[:, SIDE:], pair[0], pair[1][:, :SIDE]], 1)
    right = jnp.concatenate([pair[0][:, SIDE:], pair[1], after[:, :SIDE]], 1)
    transform(1, jnp.where(first, left, right))
    starts(0, 1)
    lax.fori_loop(1, groups, second, 0)
    ends(groups - 1, 1)
    swap(1).start()
    gspec[...] = jnp.zeros_like(gspec)

    def slope_of(b):
        target_loads[b].wait()
        swap(b).wait_recv()
        printed = jax.nn.sigmoid(steepness * (inten[b] + other[b] - threshold))
        target = twin[b].astype(jnp.float32)
        slope[b] = live_rows * (4.0 * steepness) * (printed - target) * printed * (1.0 - printed)

    def adjoint_start(e, b, slot):
        for k in range(local):
            tilt = slope[b] * weight_of(e, k)
            source = fields[b, e * local + k] * jnp.concatenate([tilt, tilt], 1)
            by_rows = dot(row_forward[...], stacked(source))
            hi, lo = split(jnp.concatenate([by_rows[:, :128], by_rows[:, 128:]], 0))
            sbuf[slot, k, :, 0:128] = hi
            sbuf[slot, k, :, 128:256] = lo

    def adjoint_end(e, b, slot):
        n = 2 * FREQ_R
        for k in range(local):
            found = dot(sbuf[slot, k], src_tab[0:256, :]) + dot(sbuf[slot, k, :, 0:128], src_tab[256:384, :])
            sums = [0.0] * 4
            for part in range(2):
                lanes = slice(part * 128, part * 128 + 128)
                sur, sui, svr, svi = quarters(found[part * n : part * n + n])
                ur, ui, vr, vi = (spec[e * local + k, i, :, lanes] for i in range(4))
                sums[0] += sur * ur + sui * ui
                sums[1] += sui * ur - sur * ui
                sums[2] += svr * vr + svi * vi
                sums[3] += svi * vr - svr * vi
            for i in range(4):
                gspec[b, i] += sums[i]

    def adjoint(b):
        def step(e, carry):
            adjoint_end(e - 1, b, (e - 1) % 2)
            adjoint_start(e, b, e % 2)
            return carry

        return step

    def inverse(b):
        total = unquarters(gspec[b, 0], gspec[b, 1], gspec[b, 2], gspec[b, 3])
        gwin[b] = dot(row_back[...], stacked(dot3(total, inv_hi[...], inv_lo[...])))

    def rows_of(index):
        return pl.ds(pl.multiple_of(index * chunk, chunk), chunk)

    def grad_copy(b, d):
        owner = lax.rem(j + d, parts)
        return pltpu.make_async_remote_copy(
            gwin.at[b, rows_of(owner), :], rbuf.at[b, d], g_send.at[b, d], g_recv.at[b, d],
            device_id=(t, owner), device_id_type=MESH)

    def edge_down(i):
        return pltpu.make_async_remote_copy(
            gwin.at[1, i * chunk : (i + 1) * chunk, 0:128], edge_right.at[mine_half], e_send.at[i], e_recv.at[0, mine_half],
            device_id=(down, i), device_id_type=MESH)

    def edge_up(i):
        return pltpu.make_async_remote_copy(
            gwin.at[1, i * chunk : (i + 1) * chunk, 128:256], edge_left.at[mine_half], e_send.at[i], e_recv.at[1, mine_half],
            device_id=(up, i), device_id_type=MESH)

    end = groups - 1
    slope_of(0)

    @pl.when(sends_down)
    def _():
        pl.semaphore_signal(ready, inc=1, device_id=(down, right_end), device_id_type=MESH)

    @pl.when(sends_up)
    def _():
        pl.semaphore_signal(ready, inc=1, device_id=(up, left_end), device_id_type=MESH)

    adjoint_start(0, 0, 0)
    lax.fori_loop(1, groups, adjoint(0), 0)
    slope_of(1)
    adjoint_end(end, 0, end % 2)
    adjoint_start(0, 1, 0)
    inverse(0)

    for d in range(1, parts):
        grad_copy(0, d).start()
    lax.fori_loop(1, groups, adjoint(1), 0)
    adjoint_end(end, 1, end % 2)
    inverse(1)

    @pl.when(sends_down)
    def _():
        pl.semaphore_wait(ready, 1)
        for i in range(parts):
            edge_down(i).start()

    @pl.when(sends_up)
    def _():
        pl.semaphore_wait(ready, 1)
        for i in range(parts):
            edge_up(i).start()

    for d in range(1, parts):
        grad_copy(1, d).start()

    def span(source, b):
        group = columns_of(source)
        return pl.ds(pl.multiple_of((2 * group + block_at(group, b)) * 128, 128), 256)

    acc[...] = jnp.zeros_like(acc)
    for b in range(2):
        acc[:, span(j, b)] += gwin[b, rows_of(j), :]
        for d in range(1, parts):
            grad_copy(b, d).wait_recv()
            acc[:, span(lax.rem(j + parts - d, parts), b)] += rbuf[b, d]

    @pl.when(has_up)
    def _():
        for side in range(2):
            pltpu.make_async_copy(edge_right.at[side], edge_right.at[side], e_recv.at[0, side]).wait()
        acc[:, BLOCK * parts :] += edge_right[0] + edge_right[1]

    @pl.when(has_down)
    def _():
        for side in range(2):
            pltpu.make_async_copy(edge_left.at[side], edge_left.at[side], e_recv.at[1, side]).wait()
        acc[:, 0:128] += edge_left[0] + edge_left[1]

    mine = jnp.where(j < groups, flag(0), flag(1))
    out_ref[...] = acc[:, SIDE : SIDE + BLOCK * parts] * mine

    for slot in range(1, groups):
        kern_copy(slot).wait_send()
    for b in range(2):
        swap(b).wait_send()
        for d in range(1, parts):
            grad_copy(b, d).wait_send()

    @pl.when(sends_down)
    def _():
        for i in range(parts):
            edge_down(i).wait_send()

    @pl.when(sends_up)
    def _():
        for i in range(parts):
            edge_up(i).wait_send()


def shards(mask_field, target_image, kernels, kernel_weights, live_list, live_count):
    strips, parts = lax.axis_size("tile"), lax.axis_size("kern")
    local = kernels.shape[0]
    groups = parts // 2
    count = local * groups
    vmem = pl.BlockSpec(memory_space=pltpu.VMEM)
    smem = pl.BlockSpec(memory_space=pltpu.SMEM)
    hbm = pl.BlockSpec(memory_space=pl.ANY)
    f32, bf16 = jnp.float32, jnp.bfloat16
    dma = pltpu.SemaphoreType.DMA
    chunk = ROWS // parts
    consts = tables()
    kernels = jnp.transpose(kernels, (0, 2, 1, 3))
    return pl.pallas_call(
        functools.partial(body, strips, parts, local),
        out_shape=jax.ShapeDtypeStruct((chunk, BLOCK * parts), f32),
        in_specs=[hbm, hbm, hbm, smem, smem, smem] + [hbm] * len(consts),
        out_specs=vmem,
        scratch_shapes=[pltpu.VMEM(c.shape, bf16) for c in consts]
        + [
            pltpu.VMEM((2, local, 6 * FREQ_R, 256), bf16),
            pltpu.VMEM((2, local, 4 * FREQ_R, 256), bf16),
            pltpu.VMEM(kernels.shape, f32),
            pltpu.VMEM((4, ROWS, 128), f32),
            pltpu.VMEM((2, ROWS, 128), jnp.int32),
            dma((7,)),
            dma((len(consts),)),
            pltpu.VMEM((groups, 64 * local, 128), f32),
            pltpu.VMEM((ROWS, 128), f32),
            pltpu.VMEM((ROWS, 128), f32),
            pltpu.VMEM((ROWS, 128), f32),
            pltpu.VMEM((2, 4, FREQ_R, FREQ_C), f32),
            pltpu.VMEM((count, 4, FREQ_R, 2 * FREQ_C), f32),
            pltpu.VMEM((2, count, ROWS, 256), f32),
            pltpu.VMEM((2, ROWS, 128), f32),
            pltpu.VMEM((2, ROWS, 128), f32),
            pltpu.VMEM((2, ROWS, 128), f32),
            pltpu.VMEM((2, 4, FREQ_R, FREQ_C), f32),
            pltpu.VMEM((2, ROWS, 256), f32),
            pltpu.VMEM((2, parts, chunk, 256), f32),
            pltpu.VMEM((2, chunk, 128), f32),
            pltpu.VMEM((2, chunk, 128), f32),
            pltpu.VMEM((chunk, BLOCK * parts + 128), f32),
            pltpu.SemaphoreType.REGULAR,
            dma((groups,)),
            dma((groups,)),
            dma((1,)),
            dma((1,)),
            dma((2,)),
            dma((2,)),
            dma((2, parts)),
            dma((2, parts)),
            dma((parts,)),
            dma((2, 2)),
        ],
        compiler_params=pltpu.CompilerParams(
            collective_id=0, has_side_effects=True, vmem_limit_bytes=56 * 1024 * 1024
        ),
    )(mask_field, target_image, kernels, kernel_weights, live_list, live_count, *consts)


def solution(mesh):
    placed = (
        P(None, "tile"),
        P(None, "tile"),
        P("kern", None, None, None),
        P("kern"),
        P("tile", None),
        P("tile"),
    )
    return jax.shard_map(
        shards, mesh=mesh, in_specs=placed, out_specs=P("kern", "tile"), check_vma=False
    )
```

```python
import functools

import jax
import jax.numpy as jnp
import ml_dtypes
import numpy as np
from jax import lax
from jax.experimental import pallas as pl
from jax.experimental.pallas import tpu as pltpu
from jax.sharding import PartitionSpec as P

MESH = pl.DeviceIdType.MESH
steepness = 4.0
threshold = 0.6

ROWS = 128
BLOCK = 128
RIM = 30
SUP = 61
PERIOD_R = 159
FREQ_R = 80
PERIOD_C = 255
FREQ_C = 128
SIDE = 64


def split_np(table):
    hi = table.astype(np.float32).astype(ml_dtypes.bfloat16)
    lo = (table - hi.astype(np.float64)).astype(np.float32).astype(ml_dtypes.bfloat16)
    return hi, lo


def phases(first, second, period):
    angle = 2.0 * np.pi / period * (np.outer(first, second) % period)
    return np.cos(angle), np.sin(angle)


@functools.cache
def tables():
    fr, fc = np.arange(FREQ_R), np.arange(FREQ_C)
    rows, window = np.arange(ROWS), np.arange(2 * BLOCK)
    taps = np.arange(SUP) - RIM
    row_weight = np.where(fr == 0, 1.0, 2.0) / PERIOD_R
    col_weight = np.where(fc == 0, 1.0, 2.0) / PERIOD_C * 0.5
    c, s = phases(fr, rows, PERIOD_R)
    to_rows_hi, to_rows_lo = split_np(np.concatenate([c, s], 0))
    row_forward = np.concatenate([to_rows_hi, to_rows_hi, to_rows_lo], 1)
    back = np.concatenate([c * row_weight[:, None], s * row_weight[:, None]], 0).T
    back_hi, back_lo = split_np(back)
    row_back = np.concatenate([back_hi, back_hi, back_lo], 1)
    c, s = phases(window, fc, PERIOD_C)
    col_hi, col_lo = split_np(np.concatenate([c, s], 1))
    inv = np.concatenate([(c * col_weight).T, (s * col_weight).T], 0)
    inv_hi, inv_lo = split_np(inv)
    mid = slice(SIDE, SIDE + BLOCK)
    inv_mid = np.concatenate([inv_hi[:, mid], inv_lo[:, mid]], 1)
    src_hi = np.concatenate([col_hi[mid], col_hi[mid], col_lo[mid]], 0)
    c, s = phases(taps, fc, PERIOD_C)
    tap_cols = np.zeros((64, 2 * FREQ_C))
    tap_cols[:SUP] = np.concatenate([c, s], 1)
    tc_hi, tc_lo = split_np(tap_cols)
    zero = np.zeros_like(tc_hi)
    tap_real = np.concatenate([tc_hi, tc_hi, tc_lo, zero], 0)
    tap_imag = np.concatenate([tc_hi, tc_hi, zero, tc_lo], 0)
    c, s = phases(fr, taps, PERIOD_R)
    tap_rows = np.zeros((2 * FREQ_R, 64))
    tap_rows[:, :SUP] = np.concatenate([c, s], 0)
    tr_hi, tr_lo = split_np(tap_rows)
    tap_row = np.concatenate([tr_hi, tr_hi, tr_lo], 1)
    return (row_forward, row_back, col_hi, col_lo, inv_hi, inv_lo, inv_mid, src_hi, tap_real, tap_imag, tap_row)


def split(value):
    hi = value.astype(jnp.bfloat16)
    lo = (value - hi.astype(jnp.float32)).astype(jnp.bfloat16)
    return hi, lo


def dot(a, b):
    return jnp.dot(a, b, preferred_element_type=jnp.float32)


def dot3(a, b_hi, b_lo):
    a_hi, a_lo = split(a)
    return dot(a_hi, b_hi) + (dot(a_lo, b_hi) + dot(a_hi, b_lo))


def stacked(value):
    hi, lo = split(value)
    return jnp.concatenate([hi, lo, hi], 0)


def quarters(spec):
    cc, cs = spec[:FREQ_R, :FREQ_C], spec[:FREQ_R, FREQ_C:]
    sc, ss = spec[FREQ_R:, :FREQ_C], spec[FREQ_R:, FREQ_C:]
    return cc - ss, cs + sc, cc + ss, sc - cs


def unquarters(ur, ui, vr, vi):
    top = jnp.concatenate([ur + vr, ui - vi], 1)
    bottom = jnp.concatenate([ui + vi, vr - ur], 1)
    return jnp.concatenate([top, bottom], 0)


def body(
    strips, parts, local,
    mask_ref, target_ref, kern_ref, weight_ref, list_ref, count_ref, *rest,
):
    table_count = len(tables())
    in_hbm, rest = rest[:table_count], rest[table_count:]
    out_ref, rest = rest[0], rest[1:]
    held, rest = rest[:table_count], rest[table_count:]
    run(strips, parts, local, mask_ref, target_ref, kern_ref, weight_ref, list_ref, count_ref, in_hbm, out_ref, held, *rest)


def run(
    strips, parts, local,
    mask_ref, target_ref, kern_ref, weight_ref, list_ref, count_ref, in_hbm, out_ref, held,
    zbuf, sbuf, raw, mwin, twin, l_sem, t_sem,
    kbuf, halo_src, halo_left, halo_right, xspec, spec, fields, inten, other, slope, gspec, gwin, rbuf,
    edge_left, edge_right, acc,
    ready, k_send, k_recv, h_send, h_recv, p_send, p_recv, g_send, g_recv, e_send, e_recv,
):
    t = lax.axis_index("tile")
    j = lax.axis_index("kern")
    up = lax.rem(t + 1, strips)
    down = lax.rem(t + strips - 1, strips)
    chunk = ROWS // parts
    groups = parts // 2

    def columns_of(device):
        return 2 * lax.rem((device // 2 + 1) // 2, 2) + lax.rem(device, 2)

    def device_of(half, columns):
        inner = columns // 2
        return 2 * (inner + half * (3 - 2 * inner)) + lax.rem(columns, 2)

    mine_half, x = j // 4, columns_of(j)
    first, last = x == 0, x == groups - 1
    has_up, has_down = t < strips - 1, t > 0
    sends_up, sends_down = last & has_up, first & has_down
    left_end, right_end = device_of(mine_half, 0), device_of(mine_half, groups - 1)
    row_forward, row_back, col_hi, col_lo, inv_hi, inv_lo, inv_mid, src_tab, tap_real, tap_imag, tap_row = held

    def strip_column(ref, index):
        return ref.at[:, pl.ds(pl.multiple_of(index * 128, 128), 128)]

    def block_at(group, turn):
        return jnp.where(group == 0, 1 - turn, turn)

    kern_load = pltpu.make_async_copy(kern_ref, raw, l_sem.at[0])
    kern_load.start()

    x_hi, x_lo = x // 2, lax.rem(x, 2)
    peers = [x, 2 * (1 - x_hi) + x_lo, 2 * x_hi + 1 - x_lo, 2 * (1 - x_hi) + 1 - x_lo]

    barrier = pltpu.get_barrier_semaphore()
    greeted = [device_of(mine_half, peer) for peer in peers[1:]] + [device_of(1 - mine_half, x)]
    for device in greeted:
        pl.semaphore_signal(barrier, inc=1, device_id=(t, device), device_id_type=MESH)

    @pl.when(sends_up)
    def _():
        pl.semaphore_signal(barrier, inc=1, device_id=(up, left_end), device_id_type=MESH)

    @pl.when(sends_down)
    def _():
        pl.semaphore_signal(barrier, inc=1, device_id=(down, right_end), device_id_type=MESH)

    at = 2 * x
    places = (jnp.maximum(at - 1, 0), at, at + 1, jnp.minimum(at + 2, parts - 1))
    loads = [
        pltpu.make_async_copy(strip_column(mask_ref, place), mwin.at[i], l_sem.at[1 + i])
        for i, place in enumerate(places)
    ]
    target_loads = [
        pltpu.make_async_copy(strip_column(target_ref, at + block_at(x, b)), twin.at[b], l_sem.at[5 + b])
        for b in range(2)
    ]
    table_loads = [
        pltpu.make_async_copy(source, place, t_sem.at[i]) for i, (source, place) in enumerate(zip(in_hbm, held))
    ]
    for load in loads + table_loads + target_loads:
        load.start()

    kbuf[0] = jnp.zeros_like(kbuf[0])
    kern_load.wait()
    for k in range(local):
        kbuf[0, 64 * k : 64 * k + SUP, 0:SUP] = raw[k, :, 0, :]
        kbuf[0, 64 * k : 64 * k + SUP, 64 : 64 + SUP] = raw[k, :, 1, :]
        kbuf[0, 64 * k + SUP : 64 * k + SUP + 1, :] = jnp.full((1, 128), weight_ref[k], jnp.float32)

    def flag(slot):
        found = jnp.float32(0.0)
        for place in range(2):
            hit = (list_ref[0, place] == slot) & (place < count_ref[0])
            found = jnp.where(hit, jnp.float32(1.0), found)
        return found

    half = ROWS // 2
    live_rows = jnp.concatenate(
        [jnp.full((half, 128), flag(0), jnp.float32), jnp.full((half, 128), flag(1), jnp.float32)], 0
    )

    edge_device = sends_up | sends_down

    @pl.when(edge_device)
    def _():
        pl.semaphore_wait(barrier, len(greeted) + 1)

    @pl.when(jnp.logical_not(edge_device))
    def _():
        pl.semaphore_wait(barrier, len(greeted))

    def to_down():
        return pltpu.make_async_remote_copy(
            halo_src, halo_right, h_send.at[0], h_recv.at[0],
            device_id=(down, right_end), device_id_type=MESH)

    def to_up():
        return pltpu.make_async_remote_copy(
            halo_src, halo_left, h_send.at[0], h_recv.at[0],
            device_id=(up, left_end), device_id_type=MESH)

    def kern_copy(slot, peer=peers[1]):
        return pltpu.make_async_remote_copy(
            kbuf.at[0], kbuf.at[slot], k_send.at[slot], k_recv.at[slot],
            device_id=(t, device_of(mine_half, peer)), device_id_type=MESH)

    for slot in range(1, groups):
        kern_copy(slot, peers[slot]).start()

    for load in loads:
        load.wait()
    halo_src[...] = jnp.where(first, mwin[1], mwin[2]) * live_rows

    @pl.when(sends_down)
    def _():
        to_down().start()

    @pl.when(sends_up)
    def _():
        to_up().start()

    for load in table_loads:
        load.wait()
    low_lanes = lax.broadcasted_iota(jnp.int32, (2 * FREQ_R, 128), 1) < 64

    def spectra(e):
        kernels = stacked(jnp.concatenate([kbuf[e, 64 * k : 64 * k + 64, :] for k in range(local)], 1))
        by_rows = dot(tap_row[...], kernels)
        for k in range(local):
            place = e * local + k
            taken = by_rows[:, 128 * k : 128 * k + 128]
            high = taken.astype(jnp.bfloat16)
            high_wide = high.astype(jnp.float32)
            low = taken - high_wide
            real = jnp.where(low_lanes, high_wide, pltpu.roll(low, 64, 1)).astype(jnp.bfloat16)
            imag = jnp.where(low_lanes, pltpu.roll(high_wide, 64, 1), low).astype(jnp.bfloat16)
            for part, (own, table) in enumerate(((real, tap_real), (imag, tap_imag))):
                lanes = slice(part * 128, part * 128 + 128)
                pieces = quarters(dot(jnp.concatenate([own, high], 1), table[...]))
                for i, piece in enumerate(pieces):
                    spec[place, i, :, lanes] = piece

    def weight_of(e, k):
        return kbuf[e, 64 * k + SUP : 64 * k + SUP + 1, :]

    def starts(e, b):
        n = 2 * FREQ_R
        for k in range(local):
            products = []
            for part in range(2):
                lanes = slice(part * 128, part * 128 + 128)
                ur, ui, vr, vi = (spec[e * local + k, i, :, lanes] for i in range(4))
                xur, xui, xvr, xvi = (xspec[b, i] for i in range(4))
                products.append(
                    unquarters(
                        ur * xur - ui * xui, ur * xui + ui * xur,
                        vr * xvr - vi * xvi, vr * xvi + vi * xvr,
                    )
                )
            y_hi, y_lo = split(jnp.concatenate(products, 0))
            wide = dot(y_hi, inv_mid[...])
            inner = wide[:, :128] + (wide[:, 128:] + dot(y_lo, inv_mid[:, :128]))
            zbuf[b, k] = stacked(jnp.concatenate([inner[:n], inner[n:]], 1))

    def ends(e, b):
        for k in range(local):
            field = dot(row_back[...], zbuf[b, k])
            fields[b, e * local + k] = field
            real, imag = field[:, :128], field[:, 128:]
            inten[b] += weight_of(e, k) * (real * real + imag * imag)

    spectra(0)

    pair = [mwin[1] * live_rows, mwin[2] * live_rows]

    def transform(b, window):
        by_rows = dot(row_forward[...], stacked(window))
        spectrum = dot3(by_rows, col_hi[...], col_lo[...])
        for i, piece in enumerate(quarters(spectrum)):
            xspec[b, i] = piece

    before, after = mwin[0] * live_rows, mwin[3] * live_rows
    left = jnp.concatenate([before[:, SIDE:], pair[0], pair[1][:, :SIDE]], 1)
    right = jnp.concatenate([pair[0][:, SIDE:], pair[1], after[:, :SIDE]], 1)
    transform(0, jnp.where(first, right, left))
    inten[...] = jnp.zeros_like(inten)

    def forward(e, carry):
        ends(e - 1, 0)
        kern_copy(e).wait_recv()
        spectra(e)
        starts(e, 0)
        return carry

    def second(e, carry):
        ends(e - 1, 1)
        starts(e, 1)
        return carry

    def swap(b):
        return pltpu.make_async_remote_copy(
            inten.at[b], other.at[b], p_send.at[b], p_recv.at[b],
            device_id=(t, device_of(1 - mine_half, x)), device_id_type=MESH)

    starts(0, 0)
    lax.fori_loop(1, groups, forward, 0, unroll=True)
    ends(groups - 1, 0)
    swap(0).start()

    @pl.when(sends_down)
    def _():
        to_down().wait()

    @pl.when(sends_up)
    def _():
        to_up().wait()

    before = jnp.where(has_down, halo_left[...], 0.0)
    after = jnp.where(last, jnp.where(has_up, halo_right[...], 0.0), mwin[3] * live_rows)
    left = jnp.concatenate([before[:, SIDE:], pair[0], pair[1][:, :SIDE]], 1)
    right = jnp.concatenate([pair[0][:, SIDE:], pair[1], after[:, :SIDE]], 1)
    transform(1, jnp.where(first, left, right))
    starts(0, 1)
    lax.fori_loop(1, groups, second, 0, unroll=True)
    ends(groups - 1, 1)
    swap(1).start()
    gspec[...] = jnp.zeros_like(gspec)

    def slope_of(b):
        target_loads[b].wait()
        swap(b).wait_recv()
        printed = jax.nn.sigmoid(steepness * (inten[b] + other[b] - threshold))
        target = twin[b].astype(jnp.float32)
        slope[b] = live_rows * (4.0 * steepness) * (printed - target) * printed * (1.0 - printed)

    def adjoint_start(e, b, slot):
        for k in range(local):
            tilt = slope[b] * weight_of(e, k)
            source = fields[b, e * local + k] * jnp.concatenate([tilt, tilt], 1)
            by_rows = dot(row_forward[...], stacked(source))
            hi, lo = split(jnp.concatenate([by_rows[:, :128], by_rows[:, 128:]], 0))
            sbuf[slot, k, :, 0:128] = hi
            sbuf[slot, k, :, 128:256] = lo

    def adjoint_end(e, b, slot):
        n = 2 * FREQ_R
        for k in range(local):
            found = dot(sbuf[slot, k], src_tab[0:256, :]) + dot(sbuf[slot, k, :, 0:128], src_tab[256:384, :])
            sums = [0.0] * 4
            for part in range(2):
                lanes = slice(part * 128, part * 128 + 128)
                sur, sui, svr, svi = quarters(found[part * n : part * n + n])
                ur, ui, vr, vi = (spec[e * local + k, i, :, lanes] for i in range(4))
                sums[0] += sur * ur + sui * ui
                sums[1] += sui * ur - sur * ui
                sums[2] += svr * vr + svi * vi
                sums[3] += svi * vr - svr * vi
            for i in range(4):
                gspec[b, i] += sums[i]

    def adjoint(b):
        def step(e, carry):
            adjoint_end(e - 1, b, (e - 1) % 2)
            adjoint_start(e, b, e % 2)
            return carry

        return step

    def inverse(b):
        total = unquarters(gspec[b, 0], gspec[b, 1], gspec[b, 2], gspec[b, 3])
        gwin[b] = dot(row_back[...], stacked(dot3(total, inv_hi[...], inv_lo[...])))

    def rows_of(index):
        return pl.ds(pl.multiple_of(index * chunk, chunk), chunk)

    def grad_copy(b, d):
        owner = lax.rem(j + d, parts)
        return pltpu.make_async_remote_copy(
            gwin.at[b, rows_of(owner), :], rbuf.at[b, d], g_send.at[b, d], g_recv.at[b, d],
            device_id=(t, owner), device_id_type=MESH)

    def edge_down(i):
        return pltpu.make_async_remote_copy(
            gwin.at[1, i * chunk : (i + 1) * chunk, 0:128], edge_right.at[mine_half], e_send.at[i], e_recv.at[0, mine_half],
            device_id=(down, i), device_id_type=MESH)

    def edge_up(i):
        return pltpu.make_async_remote_copy(
            gwin.at[1, i * chunk : (i + 1) * chunk, 128:256], edge_left.at[mine_half], e_send.at[i], e_recv.at[1, mine_half],
            device_id=(up, i), device_id_type=MESH)

    end = groups - 1
    slope_of(0)

    @pl.when(sends_down)
    def _():
        pl.semaphore_signal(ready, inc=1, device_id=(down, right_end), device_id_type=MESH)

    @pl.when(sends_up)
    def _():
        pl.semaphore_signal(ready, inc=1, device_id=(up, left_end), device_id_type=MESH)

    adjoint_start(0, 0, 0)
    lax.fori_loop(1, groups, adjoint(0), 0, unroll=True)
    slope_of(1)
    adjoint_end(end, 0, end % 2)
    adjoint_start(0, 1, 0)
    inverse(0)

    for d in range(1, parts):
        grad_copy(0, d).start()
    lax.fori_loop(1, groups, adjoint(1), 0, unroll=True)
    adjoint_end(end, 1, end % 2)
    inverse(1)

    @pl.when(sends_down)
    def _():
        pl.semaphore_wait(ready, 1)
        for i in range(parts):
            edge_down(i).start()

    @pl.when(sends_up)
    def _():
        pl.semaphore_wait(ready, 1)
        for i in range(parts):
            edge_up(i).start()

    for d in range(1, parts):
        grad_copy(1, d).start()

    def span(source, b):
        group = columns_of(source)
        return pl.ds(pl.multiple_of((2 * group + block_at(group, b)) * 128, 128), 256)

    acc[...] = jnp.zeros_like(acc)
    for b in range(2):
        acc[:, span(j, b)] += gwin[b, rows_of(j), :]
        for d in range(1, parts):
            grad_copy(b, d).wait_recv()
            acc[:, span(lax.rem(j + parts - d, parts), b)] += rbuf[b, d]

    @pl.when(has_up)
    def _():
        for side in range(2):
            pltpu.make_async_copy(edge_right.at[side], edge_right.at[side], e_recv.at[0, side]).wait()
        acc[:, BLOCK * parts :] += edge_right[0] + edge_right[1]

    @pl.when(has_down)
    def _():
        for side in range(2):
            pltpu.make_async_copy(edge_left.at[side], edge_left.at[side], e_recv.at[1, side]).wait()
        acc[:, 0:128] += edge_left[0] + edge_left[1]

    mine = jnp.where(j < groups, flag(0), flag(1))
    out_ref[...] = acc[:, SIDE : SIDE + BLOCK * parts] * mine

    for slot in range(1, groups):
        kern_copy(slot).wait_send()
    for b in range(2):
        swap(b).wait_send()
        for d in range(1, parts):
            grad_copy(b, d).wait_send()

    @pl.when(sends_down)
    def _():
        for i in range(parts):
            edge_down(i).wait_send()

    @pl.when(sends_up)
    def _():
        for i in range(parts):
            edge_up(i).wait_send()


def shards(mask_field, target_image, kernels, kernel_weights, live_list, live_count):
    strips, parts = lax.axis_size("tile"), lax.axis_size("kern")
    local = kernels.shape[0]
    groups = parts // 2
    count = local * groups
    vmem = pl.BlockSpec(memory_space=pltpu.VMEM)
    smem = pl.BlockSpec(memory_space=pltpu.SMEM)
    hbm = pl.BlockSpec(memory_space=pl.ANY)
    f32, bf16 = jnp.float32, jnp.bfloat16
    dma = pltpu.SemaphoreType.DMA
    chunk = ROWS // parts
    consts = tables()
    kernels = jnp.transpose(kernels, (0, 2, 1, 3))
    return pl.pallas_call(
        functools.partial(body, strips, parts, local),
        out_shape=jax.ShapeDtypeStruct((chunk, BLOCK * parts), f32),
        in_specs=[hbm, hbm, hbm, smem, smem, smem] + [hbm] * len(consts),
        out_specs=vmem,
        scratch_shapes=[pltpu.VMEM(c.shape, bf16) for c in consts]
        + [
            pltpu.VMEM((2, local, 6 * FREQ_R, 256), bf16),
            pltpu.VMEM((2, local, 4 * FREQ_R, 256), bf16),
            pltpu.VMEM(kernels.shape, f32),
            pltpu.VMEM((4, ROWS, 128), f32),
            pltpu.VMEM((2, ROWS, 128), jnp.int32),
            dma((7,)),
            dma((len(consts),)),
            pltpu.VMEM((groups, 64 * local, 128), f32),
            pltpu.VMEM((ROWS, 128), f32),
            pltpu.VMEM((ROWS, 128), f32),
            pltpu.VMEM((ROWS, 128), f32),
            pltpu.VMEM((2, 4, FREQ_R, FREQ_C), f32),
            pltpu.VMEM((count, 4, FREQ_R, 2 * FREQ_C), f32),
            pltpu.VMEM((2, count, ROWS, 256), f32),
            pltpu.VMEM((2, ROWS, 128), f32),
            pltpu.VMEM((2, ROWS, 128), f32),
            pltpu.VMEM((2, ROWS, 128), f32),
            pltpu.VMEM((2, 4, FREQ_R, FREQ_C), f32),
            pltpu.VMEM((2, ROWS, 256), f32),
            pltpu.VMEM((2, parts, chunk, 256), f32),
            pltpu.VMEM((2, chunk, 128), f32),
            pltpu.VMEM((2, chunk, 128), f32),
            pltpu.VMEM((chunk, BLOCK * parts + 128), f32),
            pltpu.SemaphoreType.REGULAR,
            dma((groups,)),
            dma((groups,)),
            dma((1,)),
            dma((1,)),
            dma((2,)),
            dma((2,)),
            dma((2, parts)),
            dma((2, parts)),
            dma((parts,)),
            dma((2, 2)),
        ],
        compiler_params=pltpu.CompilerParams(
            collective_id=0, has_side_effects=True, vmem_limit_bytes=56 * 1024 * 1024
        ),
    )(mask_field, target_image, kernels, kernel_weights, live_list, live_count, *consts)


def solution(mesh):
    placed = (
        P(None, "tile"),
        P(None, "tile"),
        P("kern", None, None, None),
        P("kern"),
        P("tile", None),
        P("tile"),
    )
    return jax.shard_map(
        shards, mesh=mesh, in_specs=placed, out_specs=P("kern", "tile"), check_vma=False
    )
```

```python
import functools

import jax
import jax.numpy as jnp
import ml_dtypes
import numpy as np
from jax import lax
from jax.experimental import pallas as pl
from jax.experimental.pallas import tpu as pltpu
from jax.sharding import PartitionSpec as P

MESH = pl.DeviceIdType.MESH
steepness = 4.0
threshold = 0.6

ROWS = 128
BLOCK = 128
RIM = 30
SUP = 61
PERIOD_R = 159
FREQ_R = 80
PERIOD_C = 255
FREQ_C = 128
SIDE = 64


def split_np(table):
    hi = table.astype(np.float32).astype(ml_dtypes.bfloat16)
    lo = (table - hi.astype(np.float64)).astype(np.float32).astype(ml_dtypes.bfloat16)
    return hi, lo


def phases(first, second, period):
    angle = 2.0 * np.pi / period * (np.outer(first, second) % period)
    return np.cos(angle), np.sin(angle)


@functools.cache
def tables():
    fr, fc = np.arange(FREQ_R), np.arange(FREQ_C)
    rows, window = np.arange(ROWS), np.arange(2 * BLOCK)
    taps = np.arange(SUP) - RIM
    row_weight = np.where(fr == 0, 1.0, 2.0) / PERIOD_R
    col_weight = np.where(fc == 0, 1.0, 2.0) / PERIOD_C * 0.5
    c, s = phases(fr, rows, PERIOD_R)
    to_rows_hi, to_rows_lo = split_np(np.concatenate([c, s], 0))
    row_forward = np.concatenate([to_rows_hi, to_rows_hi, to_rows_lo], 1)
    back = np.concatenate([c * row_weight[:, None], s * row_weight[:, None]], 0).T
    back_hi, back_lo = split_np(back)
    row_back = np.concatenate([back_hi, back_hi, back_lo], 1)
    c, s = phases(window, fc, PERIOD_C)
    col_hi, col_lo = split_np(np.concatenate([c, s], 1))
    inv = np.concatenate([(c * col_weight).T, (s * col_weight).T], 0)
    inv_hi, inv_lo = split_np(inv)
    mid = slice(SIDE, SIDE + BLOCK)
    inv_mid = np.concatenate([inv_hi[:, mid], inv_lo[:, mid]], 1)
    src_hi = np.concatenate([col_hi[mid], col_hi[mid], col_lo[mid]], 0)
    c, s = phases(taps, fc, PERIOD_C)
    tap_cols = np.zeros((64, 2 * FREQ_C))
    tap_cols[:SUP] = np.concatenate([c, s], 1)
    tc_hi, tc_lo = split_np(tap_cols)
    zero = np.zeros_like(tc_hi)
    tap_real = np.concatenate([tc_hi, tc_hi, tc_lo, zero], 0)
    tap_imag = np.concatenate([tc_hi, tc_hi, zero, tc_lo], 0)
    c, s = phases(fr, taps, PERIOD_R)
    tap_rows = np.zeros((2 * FREQ_R, 64))
    tap_rows[:, :SUP] = np.concatenate([c, s], 0)
    tr_hi, tr_lo = split_np(tap_rows)
    tap_row = np.concatenate([tr_hi, tr_hi, tr_lo], 1)
    return (row_forward, row_back, col_hi, col_lo, inv_hi, inv_lo, inv_mid, src_hi, tap_real, tap_imag, tap_row)


def split(value):
    hi = value.astype(jnp.bfloat16)
    lo = (value - hi.astype(jnp.float32)).astype(jnp.bfloat16)
    return hi, lo


def dot(a, b):
    return jnp.dot(a, b, preferred_element_type=jnp.float32)


def dot3(a, b_hi, b_lo):
    a_hi, a_lo = split(a)
    return dot(a_hi, b_hi) + (dot(a_lo, b_hi) + dot(a_hi, b_lo))


def stacked(value):
    hi, lo = split(value)
    return jnp.concatenate([hi, lo, hi], 0)


def quarters(spec):
    cc, cs = spec[:FREQ_R, :FREQ_C], spec[:FREQ_R, FREQ_C:]
    sc, ss = spec[FREQ_R:, :FREQ_C], spec[FREQ_R:, FREQ_C:]
    return cc - ss, cs + sc, cc + ss, sc - cs


def unquarters(ur, ui, vr, vi):
    top = jnp.concatenate([ur + vr, ui - vi], 1)
    bottom = jnp.concatenate([ui + vi, vr - ur], 1)
    return jnp.concatenate([top, bottom], 0)


def body(
    strips, parts, local,
    mask_ref, target_ref, kern_ref, weight_ref, list_ref, count_ref, *rest,
):
    table_count = len(tables())
    in_hbm, rest = rest[:table_count], rest[table_count:]
    out_ref, rest = rest[0], rest[1:]
    held, rest = rest[:table_count], rest[table_count:]
    run(strips, parts, local, mask_ref, target_ref, kern_ref, weight_ref, list_ref, count_ref, in_hbm, out_ref, held, *rest)


def run(
    strips, parts, local,
    mask_ref, target_ref, kern_ref, weight_ref, list_ref, count_ref, in_hbm, out_ref, held,
    zbuf, sbuf, raw, mwin, twin, l_sem, t_sem,
    kbuf, halo_src, halo_left, halo_right, xspec, spec, fields, inten, other, slope, gspec, gwin, rbuf,
    edge_left, edge_right, acc,
    ready, k_send, k_recv, h_send, h_recv, p_send, p_recv, g_send, g_recv, e_send, e_recv,
):
    t = lax.axis_index("tile")
    j = lax.axis_index("kern")
    up = lax.rem(t + 1, strips)
    down = lax.rem(t + strips - 1, strips)
    chunk = ROWS // parts
    groups = parts // 2

    def columns_of(device):
        return 2 * lax.rem((device // 2 + 1) // 2, 2) + lax.rem(device, 2)

    def device_of(half, columns):
        inner = columns // 2
        return 2 * (inner + half * (3 - 2 * inner)) + lax.rem(columns, 2)

    mine_half, x = j // 4, columns_of(j)
    first, last = x == 0, x == groups - 1
    has_up, has_down = t < strips - 1, t > 0
    sends_up, sends_down = last & has_up, first & has_down
    left_end, right_end = device_of(mine_half, 0), device_of(mine_half, groups - 1)
    row_forward, row_back, col_hi, col_lo, inv_hi, inv_lo, inv_mid, src_tab, tap_real, tap_imag, tap_row = held

    def strip_column(ref, index):
        return ref.at[:, pl.ds(pl.multiple_of(index * 128, 128), 128)]

    def block_at(group, turn):
        return jnp.where(group == 0, 1 - turn, turn)

    kern_load = pltpu.make_async_copy(kern_ref, raw, l_sem.at[0])
    kern_load.start()

    x_hi, x_lo = x // 2, lax.rem(x, 2)
    peers = [x, 2 * (1 - x_hi) + x_lo, 2 * x_hi + 1 - x_lo, 2 * (1 - x_hi) + 1 - x_lo]

    barrier = pltpu.get_barrier_semaphore()
    greeted = [device_of(mine_half, peer) for peer in peers[1:]] + [device_of(1 - mine_half, x)]
    for device in greeted:
        pl.semaphore_signal(barrier, inc=1, device_id=(t, device), device_id_type=MESH)

    @pl.when(sends_up)
    def _():
        pl.semaphore_signal(barrier, inc=1, device_id=(up, left_end), device_id_type=MESH)

    @pl.when(sends_down)
    def _():
        pl.semaphore_signal(barrier, inc=1, device_id=(down, right_end), device_id_type=MESH)

    at = 2 * x
    places = (jnp.maximum(at - 1, 0), at, at + 1, jnp.minimum(at + 2, parts - 1))
    loads = [
        pltpu.make_async_copy(strip_column(mask_ref, place), mwin.at[i], l_sem.at[1 + i])
        for i, place in enumerate(places)
    ]
    target_loads = [
        pltpu.make_async_copy(strip_column(target_ref, at + block_at(x, b)), twin.at[b], l_sem.at[5 + b])
        for b in range(2)
    ]
    table_loads = [
        pltpu.make_async_copy(source, place, t_sem.at[i]) for i, (source, place) in enumerate(zip(in_hbm, held))
    ]
    for load in loads + table_loads + target_loads:
        load.start()

    kbuf[0] = jnp.zeros_like(kbuf[0])
    kern_load.wait()
    for k in range(local):
        kbuf[0, 64 * k : 64 * k + SUP, 0:SUP] = raw[k, :, 0, :]
        kbuf[0, 64 * k : 64 * k + SUP, 64 : 64 + SUP] = raw[k, :, 1, :]
        kbuf[0, 64 * k + SUP : 64 * k + SUP + 1, :] = jnp.full((1, 128), weight_ref[k], jnp.float32)

    def flag(slot):
        found = jnp.float32(0.0)
        for place in range(2):
            hit = (list_ref[0, place] == slot) & (place < count_ref[0])
            found = jnp.where(hit, jnp.float32(1.0), found)
        return found

    half = ROWS // 2
    live_rows = jnp.concatenate(
        [jnp.full((half, 128), flag(0), jnp.float32), jnp.full((half, 128), flag(1), jnp.float32)], 0
    )

    edge_device = sends_up | sends_down

    @pl.when(edge_device)
    def _():
        pl.semaphore_wait(barrier, len(greeted) + 1)

    @pl.when(jnp.logical_not(edge_device))
    def _():
        pl.semaphore_wait(barrier, len(greeted))

    def to_down():
        return pltpu.make_async_remote_copy(
            halo_src, halo_right, h_send.at[0], h_recv.at[0],
            device_id=(down, right_end), device_id_type=MESH)

    def to_up():
        return pltpu.make_async_remote_copy(
            halo_src, halo_left, h_send.at[0], h_recv.at[0],
            device_id=(up, left_end), device_id_type=MESH)

    def kern_copy(slot, peer=peers[1]):
        return pltpu.make_async_remote_copy(
            kbuf.at[0], kbuf.at[slot], k_send.at[slot], k_recv.at[slot],
            device_id=(t, device_of(mine_half, peer)), device_id_type=MESH)

    for slot in range(1, groups):
        kern_copy(slot, peers[slot]).start()

    for load in loads:
        load.wait()
    halo_src[...] = jnp.where(first, mwin[1], mwin[2]) * live_rows

    @pl.when(sends_down)
    def _():
        to_down().start()

    @pl.when(sends_up)
    def _():
        to_up().start()

    for load in table_loads[8:]:
        load.wait()
    low_lanes = lax.broadcasted_iota(jnp.int32, (2 * FREQ_R, 128), 1) < 64

    def spectra(e):
        kernels = stacked(jnp.concatenate([kbuf[e, 64 * k : 64 * k + 64, :] for k in range(local)], 1))
        by_rows = dot(tap_row[...], kernels)
        for k in range(local):
            place = e * local + k
            taken = by_rows[:, 128 * k : 128 * k + 128]
            high = taken.astype(jnp.bfloat16)
            high_wide = high.astype(jnp.float32)
            low = taken - high_wide
            real = jnp.where(low_lanes, high_wide, pltpu.roll(low, 64, 1)).astype(jnp.bfloat16)
            imag = jnp.where(low_lanes, pltpu.roll(high_wide, 64, 1), low).astype(jnp.bfloat16)
            for part, (own, table) in enumerate(((real, tap_real), (imag, tap_imag))):
                lanes = slice(part * 128, part * 128 + 128)
                pieces = quarters(dot(jnp.concatenate([own, high], 1), table[...]))
                for i, piece in enumerate(pieces):
                    spec[place, i, :, lanes] = piece

    def weight_of(e, k):
        return kbuf[e, 64 * k + SUP : 64 * k + SUP + 1, :]

    def starts(e, b):
        n = 2 * FREQ_R
        for k in range(local):
            products = []
            for part in range(2):
                lanes = slice(part * 128, part * 128 + 128)
                ur, ui, vr, vi = (spec[e * local + k, i, :, lanes] for i in range(4))
                xur, xui, xvr, xvi = (xspec[b, i] for i in range(4))
                products.append(
                    unquarters(
                        ur * xur - ui * xui, ur * xui + ui * xur,
                        vr * xvr - vi * xvi, vr * xvi + vi * xvr,
                    )
                )
            y_hi, y_lo = split(jnp.concatenate(products, 0))
            wide = dot(y_hi, inv_mid[...])
            inner = wide[:, :128] + (wide[:, 128:] + dot(y_lo, inv_mid[:, :128]))
            zbuf[b, k] = stacked(jnp.concatenate([inner[:n], inner[n:]], 1))

    def ends(e, b):
        for k in range(local):
            field = dot(row_back[...], zbuf[b, k])
            fields[b, e * local + k] = field
            real, imag = field[:, :128], field[:, 128:]
            inten[b] += weight_of(e, k) * (real * real + imag * imag)

    spectra(0)
    for load in table_loads[:8]:
        load.wait()

    pair = [mwin[1] * live_rows, mwin[2] * live_rows]

    def transform(b, window):
        by_rows = dot(row_forward[...], stacked(window))
        spectrum = dot3(by_rows, col_hi[...], col_lo[...])
        for i, piece in enumerate(quarters(spectrum)):
            xspec[b, i] = piece

    before, after = mwin[0] * live_rows, mwin[3] * live_rows
    left = jnp.concatenate([before[:, SIDE:], pair[0], pair[1][:, :SIDE]], 1)
    right = jnp.concatenate([pair[0][:, SIDE:], pair[1], after[:, :SIDE]], 1)
    transform(0, jnp.where(first, right, left))
    inten[...] = jnp.zeros_like(inten)

    def forward(e, carry):
        ends(e - 1, 0)
        kern_copy(e).wait_recv()
        spectra(e)
        starts(e, 0)
        return carry

    def second(e, carry):
        ends(e - 1, 1)
        starts(e, 1)
        return carry

    def swap(b):
        return pltpu.make_async_remote_copy(
            inten.at[b], other.at[b], p_send.at[b], p_recv.at[b],
            device_id=(t, device_of(1 - mine_half, x)), device_id_type=MESH)

    starts(0, 0)
    lax.fori_loop(1, groups, forward, 0, unroll=True)
    ends(groups - 1, 0)
    swap(0).start()

    @pl.when(sends_down)
    def _():
        to_down().wait()

    @pl.when(sends_up)
    def _():
        to_up().wait()

    before = jnp.where(has_down, halo_left[...], 0.0)
    after = jnp.where(last, jnp.where(has_up, halo_right[...], 0.0), mwin[3] * live_rows)
    left = jnp.concatenate([before[:, SIDE:], pair[0], pair[1][:, :SIDE]], 1)
    right = jnp.concatenate([pair[0][:, SIDE:], pair[1], after[:, :SIDE]], 1)
    transform(1, jnp.where(first, left, right))
    starts(0, 1)
    lax.fori_loop(1, groups, second, 0, unroll=True)
    ends(groups - 1, 1)
    swap(1).start()
    gspec[...] = jnp.zeros_like(gspec)

    def slope_of(b):
        target_loads[b].wait()
        swap(b).wait_recv()
        printed = jax.nn.sigmoid(steepness * (inten[b] + other[b] - threshold))
        target = twin[b].astype(jnp.float32)
        slope[b] = live_rows * (4.0 * steepness) * (printed - target) * printed * (1.0 - printed)

    def adjoint_start(e, b, slot):
        for k in range(local):
            tilt = slope[b] * weight_of(e, k)
            source = fields[b, e * local + k] * jnp.concatenate([tilt, tilt], 1)
            by_rows = dot(row_forward[...], stacked(source))
            hi, lo = split(jnp.concatenate([by_rows[:, :128], by_rows[:, 128:]], 0))
            sbuf[slot, k, :, 0:128] = hi
            sbuf[slot, k, :, 128:256] = lo

    def adjoint_end(e, b, slot):
        n = 2 * FREQ_R
        for k in range(local):
            found = dot(sbuf[slot, k], src_tab[0:256, :]) + dot(sbuf[slot, k, :, 0:128], src_tab[256:384, :])
            sums = [0.0] * 4
            for part in range(2):
                lanes = slice(part * 128, part * 128 + 128)
                sur, sui, svr, svi = quarters(found[part * n : part * n + n])
                ur, ui, vr, vi = (spec[e * local + k, i, :, lanes] for i in range(4))
                sums[0] += sur * ur + sui * ui
                sums[1] += sui * ur - sur * ui
                sums[2] += svr * vr + svi * vi
                sums[3] += svi * vr - svr * vi
            for i in range(4):
                gspec[b, i] += sums[i]

    def adjoint(b):
        def step(e, carry):
            adjoint_end(e - 1, b, (e - 1) % 2)
            adjoint_start(e, b, e % 2)
            return carry

        return step

    def inverse(b):
        total = unquarters(gspec[b, 0], gspec[b, 1], gspec[b, 2], gspec[b, 3])
        gwin[b] = dot(row_back[...], stacked(dot3(total, inv_hi[...], inv_lo[...])))

    def rows_of(index):
        return pl.ds(pl.multiple_of(index * chunk, chunk), chunk)

    def grad_copy(b, d):
        owner = lax.rem(j + d, parts)
        return pltpu.make_async_remote_copy(
            gwin.at[b, rows_of(owner), :], rbuf.at[b, d], g_send.at[b, d], g_recv.at[b, d],
            device_id=(t, owner), device_id_type=MESH)

    def edge_down(i):
        return pltpu.make_async_remote_copy(
            gwin.at[1, i * chunk : (i + 1) * chunk, 0:128], edge_right.at[mine_half], e_send.at[i], e_recv.at[0, mine_half],
            device_id=(down, i), device_id_type=MESH)

    def edge_up(i):
        return pltpu.make_async_remote_copy(
            gwin.at[1, i * chunk : (i + 1) * chunk, 128:256], edge_left.at[mine_half], e_send.at[i], e_recv.at[1, mine_half],
            device_id=(up, i), device_id_type=MESH)

    end = groups - 1
    slope_of(0)

    @pl.when(sends_down)
    def _():
        pl.semaphore_signal(ready, inc=1, device_id=(down, right_end), device_id_type=MESH)

    @pl.when(sends_up)
    def _():
        pl.semaphore_signal(ready, inc=1, device_id=(up, left_end), device_id_type=MESH)

    adjoint_start(0, 0, 0)
    lax.fori_loop(1, groups, adjoint(0), 0, unroll=True)
    slope_of(1)
    adjoint_end(end, 0, end % 2)
    adjoint_start(0, 1, 0)
    inverse(0)

    for d in range(1, parts):
        grad_copy(0, d).start()
    lax.fori_loop(1, groups, adjoint(1), 0, unroll=True)
    adjoint_end(end, 1, end % 2)
    inverse(1)

    for d in range(1, parts):
        grad_copy(1, d).start()

    @pl.when(sends_down)
    def _():
        pl.semaphore_wait(ready, 1)
        for i in range(parts):
            edge_down(i).start()

    @pl.when(sends_up)
    def _():
        pl.semaphore_wait(ready, 1)
        for i in range(parts):
            edge_up(i).start()

    def span(source, b):
        group = columns_of(source)
        return pl.ds(pl.multiple_of((2 * group + block_at(group, b)) * 128, 128), 256)

    acc[...] = jnp.zeros_like(acc)
    for b in range(2):
        acc[:, span(j, b)] += gwin[b, rows_of(j), :]
        for d in range(1, parts):
            grad_copy(b, d).wait_recv()
            acc[:, span(lax.rem(j + parts - d, parts), b)] += rbuf[b, d]

    @pl.when(has_up)
    def _():
        for side in range(2):
            pltpu.make_async_copy(edge_right.at[side], edge_right.at[side], e_recv.at[0, side]).wait()
        acc[:, BLOCK * parts :] += edge_right[0] + edge_right[1]

    @pl.when(has_down)
    def _():
        for side in range(2):
            pltpu.make_async_copy(edge_left.at[side], edge_left.at[side], e_recv.at[1, side]).wait()
        acc[:, 0:128] += edge_left[0] + edge_left[1]

    mine = jnp.where(j < groups, flag(0), flag(1))
    out_ref[...] = acc[:, SIDE : SIDE + BLOCK * parts] * mine

    for slot in range(1, groups):
        kern_copy(slot).wait_send()
    for b in range(2):
        swap(b).wait_send()
        for d in range(1, parts):
            grad_copy(b, d).wait_send()

    @pl.when(sends_down)
    def _():
        for i in range(parts):
            edge_down(i).wait_send()

    @pl.when(sends_up)
    def _():
        for i in range(parts):
            edge_up(i).wait_send()


def shards(mask_field, target_image, kernels, kernel_weights, live_list, live_count):
    strips, parts = lax.axis_size("tile"), lax.axis_size("kern")
    local = kernels.shape[0]
    groups = parts // 2
    count = local * groups
    vmem = pl.BlockSpec(memory_space=pltpu.VMEM)
    smem = pl.BlockSpec(memory_space=pltpu.SMEM)
    hbm = pl.BlockSpec(memory_space=pl.ANY)
    f32, bf16 = jnp.float32, jnp.bfloat16
    dma = pltpu.SemaphoreType.DMA
    chunk = ROWS // parts
    consts = tables()
    kernels = jnp.transpose(kernels, (0, 2, 1, 3))
    return pl.pallas_call(
        functools.partial(body, strips, parts, local),
        out_shape=jax.ShapeDtypeStruct((chunk, BLOCK * parts), f32),
        in_specs=[hbm, hbm, hbm, smem, smem, smem] + [hbm] * len(consts),
        out_specs=vmem,
        scratch_shapes=[pltpu.VMEM(c.shape, bf16) for c in consts]
        + [
            pltpu.VMEM((2, local, 6 * FREQ_R, 256), bf16),
            pltpu.VMEM((2, local, 4 * FREQ_R, 256), bf16),
            pltpu.VMEM(kernels.shape, f32),
            pltpu.VMEM((4, ROWS, 128), f32),
            pltpu.VMEM((2, ROWS, 128), jnp.int32),
            dma((7,)),
            dma((len(consts),)),
            pltpu.VMEM((groups, 64 * local, 128), f32),
            pltpu.VMEM((ROWS, 128), f32),
            pltpu.VMEM((ROWS, 128), f32),
            pltpu.VMEM((ROWS, 128), f32),
            pltpu.VMEM((2, 4, FREQ_R, FREQ_C), f32),
            pltpu.VMEM((count, 4, FREQ_R, 2 * FREQ_C), f32),
            pltpu.VMEM((2, count, ROWS, 256), f32),
            pltpu.VMEM((2, ROWS, 128), f32),
            pltpu.VMEM((2, ROWS, 128), f32),
            pltpu.VMEM((2, ROWS, 128), f32),
            pltpu.VMEM((2, 4, FREQ_R, FREQ_C), f32),
            pltpu.VMEM((2, ROWS, 256), f32),
            pltpu.VMEM((2, parts, chunk, 256), f32),
            pltpu.VMEM((2, chunk, 128), f32),
            pltpu.VMEM((2, chunk, 128), f32),
            pltpu.VMEM((chunk, BLOCK * parts + 128), f32),
            pltpu.SemaphoreType.REGULAR,
            dma((groups,)),
            dma((groups,)),
            dma((1,)),
            dma((1,)),
            dma((2,)),
            dma((2,)),
            dma((2, parts)),
            dma((2, parts)),
            dma((parts,)),
            dma((2, 2)),
        ],
        compiler_params=pltpu.CompilerParams(
            collective_id=0, has_side_effects=True, vmem_limit_bytes=56 * 1024 * 1024
        ),
    )(mask_field, target_image, kernels, kernel_weights, live_list, live_count, *consts)


def solution(mesh):
    placed = (
        P(None, "tile"),
        P(None, "tile"),
        P("kern", None, None, None),
        P("kern"),
        P("tile", None),
        P("tile"),
    )
    return jax.shard_map(
        shards, mesh=mesh, in_specs=placed, out_specs=P("kern", "tile"), check_vma=False
    )
```
